256 devices in a mesh: grp: 8 (over x_hi, y), blk: 32 (over z, x_lo, core).
Axes of the slice: x: 4 (x_hi: 2, x_lo: 2; x = x_hi * 2 + x_lo), y: 4, z: 8, core: 2. Of those that a mesh axis runs over, the one named last changes fastest.
Arguments:
- residual_in: bfloat16 [512, 16384], P('grp', 'blk'), may hold values from -6 to 6
- queries: bfloat16 [512, 16384], P('grp')
- key_cache: bfloat16 [512, 32, 64, 128], P('grp', 'blk')
- value_cache: bfloat16 [512, 32, 64, 128], P('grp', 'blk'), may hold values from -6 to 6
- key_new: bfloat16 [512, 1024], P('grp'), may hold values from -6 to 6
- value_new: bfloat16 [512, 1024], P('grp'), may hold values from -6 to 6
- lengths: int32 [512], P('grp'), may hold values from 2 to 256, as said below
- ffn_gain: bfloat16 [16384], P('blk'), may hold values from 0.099609375 to 1.8984375
- gate_weight: bfloat16 [16384, 26624], P('blk', 'grp'), may hold values from -0.046875 to 0.046875
- up_weight: bfloat16 [16384, 26624], P('blk', 'grp'), may hold values from -0.046875 to 0.046875
- down_weight: bfloat16 [26624, 16384], P('grp', 'blk'), may hold values from -0.0390625 to 0.0390625
Outputs:
- layer_out: float32 [512, 16384], P('grp', 'blk')
The draws below stay inside these ranges and needn't reach their ends.
Inputs may be any that keep to these rules, and one draw needn't show every extreme that they name: `lengths`: every sequence has at least two valid cache positions, and some sequence fills all 256.
All inputs are finite; a program needn't handle non-finite values.
Results may differ from the reference program's by a relative error of at most 0.0075.
Values may be sent and summed in bfloat16 or wider, within the bound.
A program may use at most 128 MiB of HBM per device.

```python
import math
import jax
import jax.numpy as jnp
from jax import lax

D = 16384
HEADS = 128
KV_HEADS = 8
HD = 128
FF = 26624
CTX_Q = 64
B = 512
SPLIT = 4
CTX = 256
N_BLK = 32


def cache_keys(key):
    return jax.random.normal(jax.random.fold_in(key, 11), (B, KV_HEADS * SPLIT, CTX_Q, HD), jnp.float32)


def draw_key_cache(key, part):
    shared = cache_keys(key)
    return shared.astype(jnp.bfloat16)


def draw_queries(key, part):
    key = jax.random.fold_in(key, 5)
    jitter = jax.random.normal(key, (B, HEADS, HD), jnp.float32)
    values = 2.0 * jitter
    return values.reshape(B, HEADS * HD).astype(jnp.bfloat16)


def draw_lengths(key, part):
    key = jax.random.fold_in(key, 9)
    drawn = jax.random.randint(key, (B,), 2, CTX + 1, dtype=jnp.int32)
    return drawn.at[0].set(CTX).astype(jnp.int32)


def levels(stream_key, shape, shards, low, top_value):
    gain = 1.0
    for position, shards_of in shards:
        draws = jax.random.uniform(jax.random.fold_in(jax.random.fold_in(stream_key, 6), position), (shards_of,), jnp.float32, low / len(shards), top_value / len(shards))
        gain = gain * jnp.repeat(jnp.exp(draws), shape[position] // shards_of).reshape((-1,) + (1,) * (len(shape) - 1 - position))
    return gain


def noise(rng, dims, scale, limit, split=(), kind=jnp.bfloat16):
    array = jax.random.normal(rng, dims, jnp.float32) * scale
    if len(split) > 0:
        array = levels(rng, dims, split, -0.22, 0.18) * array
    return jnp.clip(array, min=-limit, max=limit).astype(kind)


def setup_inputs(seed: int = 0) -> dict:
    splits = jax.random.split(jax.random.key(seed), 12)
    return {
        "residual_in": noise(splits[0], (B, D), 0.5, 6.0, ((0, 8), (1, 32))),
        "queries": draw_queries(jax.random.fold_in(splits[11], 71), 0),
        "key_cache": draw_key_cache(jax.random.fold_in(splits[11], 71), 0),
        "value_cache": noise(splits[3], (B, KV_HEADS * SPLIT, CTX_Q, HD), 1.0, 6.0, ((0, 8), (1, 32))),
        "key_new": noise(splits[4], (B, KV_HEADS * HD), 1.0, 6.0, ((0, 8),)),
        "value_new": noise(splits[5], (B, KV_HEADS * HD), 1.0, 6.0, ((0, 8),)),
        "lengths": draw_lengths(jax.random.fold_in(splits[11], 71), 0),
        "ffn_gain": jnp.clip(1.0 + 0.18 * jax.random.normal(splits[7], (D,), jnp.float32), 0.099609375, 1.8984375).astype(jnp.bfloat16),
        "gate_weight": noise(splits[8], (D, FF), D ** -0.5, 0.046875, ((0, 32), (1, 8))),
        "up_weight": noise(splits[9], (D, FF), D ** -0.5, 0.046875, ((0, 32), (1, 8))),
        "down_weight": noise(splits[10], (FF, D), FF ** -0.5, 0.0390625, ((0, 8), (1, 32))),
    }


def attend_one(operands):
    query_row, key_rows, value_rows, key_fresh, value_fresh, length = operands
    quarters = N_BLK // KV_HEADS
    per_kv = HEADS // KV_HEADS
    score_scale = 1.0 / math.sqrt(HD)
    query_heads = query_row.astype(jnp.float32).reshape(KV_HEADS, per_kv, HD)
    keys_all = key_rows.astype(jnp.float32).reshape(KV_HEADS, quarters * CTX_Q, HD)
    values_all = value_rows.astype(jnp.float32).reshape(KV_HEADS, quarters * CTX_Q, HD)
    places = jnp.arange(quarters * CTX_Q, dtype=jnp.int32)
    usable = (places < length)[None, None, :]
    scores = jnp.einsum('khd,kpd->khp', query_heads, keys_all) * score_scale
    fresh_key = key_fresh.astype(jnp.float32).reshape(KV_HEADS, HD)
    fresh_value = value_fresh.astype(jnp.float32).reshape(KV_HEADS, 1, HD)
    fresh = jnp.einsum('khd,kd->kh', query_heads, fresh_key) * score_scale
    largest = jnp.maximum(lax.optimization_barrier(jnp.max(jnp.where(usable, scores, -jnp.inf), axis=2)), fresh)
    weights = jnp.where(usable, jnp.exp(scores - largest[..., None]), 0.0)
    fresh_weight = jnp.exp(fresh - largest)
    totals = lax.optimization_barrier(jnp.sum(weights, axis=2)) + fresh_weight
    weighted = jnp.einsum('khp,kpd->khd', weights, values_all) + fresh_weight[..., None] * fresh_value
    return (weighted / totals[..., None]).reshape(HEADS * HD)

def reference(residual_in, queries, key_cache, value_cache, key_new, value_new, lengths, ffn_gain, gate_weight, up_weight, down_weight):
    attention = lax.map(attend_one, (queries, key_cache, value_cache, key_new, value_new, lengths))
    wide = residual_in.astype(jnp.float32) + attention
    mean_square = lax.optimization_barrier(jnp.mean(wide * wide, axis=1))
    normed = (wide * ffn_gain.astype(jnp.float32)[None, :] * lax.rsqrt(mean_square + 1e-05)[:, None]).astype(jnp.bfloat16)
    gate = jnp.dot(normed, gate_weight, preferred_element_type=jnp.float32)
    up_part = jnp.dot(normed, up_weight, preferred_element_type=jnp.float32)
    hidden = (jax.nn.silu(gate) * up_part).astype(jnp.bfloat16)
    down = jnp.dot(hidden, down_weight, preferred_element_type=jnp.float32)
    return wide + down
```

```python
import functools
import math

import jax
import jax.numpy as jnp
from jax import lax
from jax.experimental import pallas as pl
from jax.experimental.pallas import tpu as pltpu
from jax.sharding import PartitionSpec as P

D = 16384
HEADS = 128
KV_HEADS = 8
MESH = pl.DeviceIdType.MESH
F32 = jnp.float32
BF16 = jnp.bfloat16

RING = 8
GROUPS = 8
FEAT = 512
HALF = 1664
WIDE = HALF + 128
C1 = 768
C2 = HALF - C1


def slot_of(distance):
    return jnp.where(distance <= 4, 8 - 2 * distance, 2 * distance - 9)


def kernel(
    w_in, st_in, res, gain, gate, up, down, out,
    w_got, st_got, wide_s, token_s, inv_gain,
    gate_w, up_w, down_w, x_s, pu, pg,
    xg_send, xg_recv, ua_send, ua_recv, ub_send, ub_recv,
    ga_send, ga_recv, gb_send, gb_recv, xu_send, xu_recv,
    h1, h2, dp, dr, ds_send, fr,
    local_sem, wsem_s, wsem_r, at_s, at_r, tok_s, tok_r, mate_s, mate_r,
    xg_ss, xg_rs, ua_ss, ua_rs, ub_ss, ub_rs, ga_ss, ga_rs, gb_ss, gb_rs, xu_ss, xu_rs,
    hz_s, hz_r, hx_s, hx_r, dr_s, dr_r, fr_s, fr_r,
):
    g = lax.axis_index("grp")
    b = lax.axis_index("blk")
    z = b // 4
    q = b % 4
    x = q // 2
    core = q % 2
    sign = 1 - 2 * core
    mate = (g, z * 4 + x * 2 + (1 - core))
    xmate = (g, z * 4 + (1 - x) * 2 + core)
    ahead = (g, lax.rem(z + sign + RING, RING) * 4 + q)
    behind = (g, lax.rem(z - sign + RING, RING) * 4 + q)
    x_other = 1 - x

    def remote(src, dst, ss, rs, to):
        return pltpu.make_async_remote_copy(
            src_ref=src, dst_ref=dst, send_sem=ss, recv_sem=rs, device_id=to, device_id_type=MESH
        )

    def peer(n):
        return (lax.rem(g // 4 + n // 4, 2)) * 4 + lax.rem(g % 4 + n % 4, 4)

    def source(n):
        return (lax.rem(g // 4 + n // 4, 2)) * 4 + lax.rem(g % 4 - n % 4 + 4, 4)

    ORDER = (1, 3, 2, 4, 5, 7, 6)

    mine = pl.ds(pl.multiple_of(core * HALF, 128), HALF)
    other = pl.ds(pl.multiple_of((1 - core) * HALF, 128), HALF)
    rows = pl.ds(pl.multiple_of(core * FEAT, FEAT), FEAT)
    loads = [
        pltpu.make_async_copy(gate.at[:, mine], gate_w.at[rows], local_sem.at[0]),
        pltpu.make_async_copy(up.at[:, mine], up_w.at[rows], local_sem.at[1]),
        pltpu.make_async_copy(down.at[mine], down_w.at[core], local_sem.at[2]),
    ]
    for load in loads:
        load.start()

    barrier = pltpu.get_barrier_semaphore()
    partners = [mate, xmate, (g, z * 4 + (1 - x) * 2 + (1 - core)), ahead, behind]
    partners += [(peer(n), b) for n in ORDER]
    for partner in partners:
        pl.semaphore_signal(barrier, inc=1, device_id=partner, device_id_type=MESH)

    inv_gain[core] = jnp.broadcast_to(1.0 / gain[...].astype(F32), (8, FEAT))
    pl.semaphore_wait(barrier, len(partners))

    merges = []
    for n in (3, 2, 1):
        p = q ^ n
        to = (g, z * 4 + p)
        merges.append(remote(st_in.at[p], st_got.at[q], at_s.at[n], at_r.at[q], to))
        merges.append(remote(w_in.at[p], w_got.at[q], at_s.at[4 + n], at_r.at[4 + q], to))
    for copy in merges:
        copy.start()
    pushes = [
        remote(inv_gain.at[core], inv_gain.at[core], wsem_s.at[0], wsem_r.at[0], mate),
        remote(up.at[:, other], up_w.at[rows], wsem_s.at[1], wsem_r.at[1], mate),
        remote(gate.at[:, other], gate_w.at[rows], wsem_s.at[2], wsem_r.at[2], mate),
        remote(down.at[other], down_w.at[core], wsem_s.at[3], wsem_r.at[3], mate),
    ]
    for push in pushes[:3]:
        push.start()
    st_got[q] = st_in[q]
    w_got[q] = w_in[q]
    for n in (1, 2, 3):
        p = q ^ n
        to = (g, z * 4 + p)
        remote(st_in.at[p], st_got.at[p], at_s.at[n], at_r.at[p], to).wait_recv()
        remote(w_in.at[p], w_got.at[p], at_s.at[4 + n], at_r.at[4 + p], to).wait_recv()
    for head in range(4):
        cols = slice(head * 128, head * 128 + 128)
        tops = [st_got[j][:, head : head + 1] for j in range(4)]
        sums = [st_got[j][:, 4 + head : 5 + head] for j in range(4)]
        top = jnp.maximum(jnp.maximum(tops[0], tops[1]), jnp.maximum(tops[2], tops[3]))
        factors = [jnp.exp(t - top) for t in tops]
        total = sum(f * s for f, s in zip(factors, sums))
        mixed = sum(f * w_got[j, :, cols].astype(F32) for j, f in enumerate(factors))
        wide = res[:, cols].astype(F32) + mixed / total
        wide_s[:, cols] = wide
        scaled = (wide * gain[:, cols].astype(F32)).astype(BF16)
        token_s[0, :, cols] = scaled[:32]
        token_s[1, :, cols] = scaled[32:]

    def slots(owner):
        away = lax.rem((owner - z) * sign + 2 * RING - 1, RING) + 1
        back = lax.rem(RING - away + RING - 1, RING) + 1
        return slot_of(away), slot_of(back)

    lanes = pl.ds(pl.multiple_of(core * FEAT, FEAT), FEAT)
    own_slot, own_mate_slot = slots(g)
    gathers = []
    for n in ORDER[::-1]:
        gathers.append(
            remote(token_s, x_s.at[own_slot, :, :, lanes], tok_s.at[n], tok_r.at[n], (peer(n), b))
        )
    for copy in gathers:
        copy.start()
    x_s[own_slot, :, :, lanes] = token_s[...]
    to_mate = [remote(token_s, x_s.at[own_mate_slot, :, :, lanes], mate_s.at[0], mate_r.at[0], mate)]
    to_mate[0].start()
    for n in ORDER:
        here, there = slots(source(n))
        remote(
            token_s, x_s.at[here, :, :, lanes], tok_s.at[n], tok_r.at[n], (peer(n), b)
        ).wait_recv()
        copy = remote(
            x_s.at[here, :, :, lanes], x_s.at[there, :, :, lanes], mate_s.at[n], mate_r.at[n], mate
        )
        copy.start()
        to_mate.append(copy)
    for load in loads[:2]:
        load.wait()
    for push in pushes[:3]:
        push.wait()
    for copy in to_mate:
        copy.wait_recv()
    pushes[3].start()

    lane = lax.broadcasted_iota(jnp.int32, (32, 128), 1)

    def project(s):
        tokens = x_s[pl.ds(s * 2, 2)].reshape(128, 2 * FEAT)
        return tokens

    def up_pair(s):
        tokens = project(s)
        for lo in range(0, HALF, 512):
            hi = min(lo + 512, HALF)
            part = jnp.dot(tokens, up_w[:, lo:hi], preferred_element_type=F32)
            pu[pl.ds(s * 2, 2), :, :, lo:hi] = part.reshape(2, 2, 32, hi - lo)
        plain = [
            tokens[:, c * FEAT : (c + 1) * FEAT].astype(F32) * inv_gain[c, 0:1] for c in range(2)
        ]
        squares = plain[0] * plain[0] + plain[1] * plain[1]
        total = jnp.sum(squares, axis=1, keepdims=True)
        pu[pl.ds(s * 2, 2), :, :, HALF:] = jnp.broadcast_to(total, (128, 128)).reshape(2, 2, 32, 128)

    def gate_pair(s):
        tokens = project(s)
        for lo in range(0, HALF, 512):
            hi = min(lo + 512, HALF)
            part = jnp.dot(tokens, gate_w[:, lo:hi], preferred_element_type=F32)
            pg[pl.ds(s * 2, 2), :, :, lo:hi] = part.reshape(2, 2, 32, hi - lo)
        xg_send[pl.ds(s * 2, 2)] = pg[pl.ds(s * 2, 2), x_other].astype(BF16)

    def xg_copy(s):
        two = pl.ds(s * 2, 2)
        return remote(xg_send.at[two], xg_recv.at[two], xg_ss.at[s], xg_rs.at[s], xmate)

    def up_sum(block, half, arrived):
        body = pu[block, half, :, :HALF]
        squares = pu[block, half, :, HALF:]
        for ref in arrived:
            body = body + ref[:, :HALF].astype(F32)
            halves = ref[:, HALF:].astype(F32)
            squares = squares + halves + pltpu.roll(halves, 64, 1)
        return body, squares

    def put_up(ref, body, squares):
        ref[:, :HALF] = body.astype(BF16)
        high = squares.astype(BF16)
        low = (squares - high.astype(F32)).astype(BF16)
        ref[:, HALF:] = jnp.where(lane < 64, high.astype(F32), low.astype(F32)).astype(BF16)

    halves = (x_other, x)
    sent = []

    def ua_copy(s, n):
        h = halves[n]
        return remote(ua_send.at[s, h], ua_recv.at[s, h], ua_ss.at[s, n], ua_rs.at[s, n], ahead)

    def ub_copy(s, n):
        h = halves[n]
        return remote(ub_send.at[s, h], ub_recv.at[s, h], ub_ss.at[s, n], ub_rs.at[s, n], behind)

    def ga_copy(s):
        return remote(ga_send.at[s], ga_recv.at[s], ga_ss.at[s], ga_rs.at[s], ahead)

    def gb_copy(s):
        return remote(gb_send.at[s], gb_recv.at[s], gb_ss.at[s], gb_rs.at[s], behind)

    def up_step(s):
        for n in range(2):
            h = halves[n]
            if s > 0:
                ua_copy(s - 1, n).wait_recv()
            arrived = [ua_recv.at[s - 1, h]] if s > 0 else []
            put_up(ua_send.at[s, h], *up_sum(2 * s, h, arrived))
            ua_copy(s, n).start()
            sent.append(ua_copy(s, n))
            if s < 3:
                if s > 0:
                    ub_copy(s - 1, n).wait_recv()
                arrived = [ub_recv.at[s - 1, h]] if s > 0 else []
                put_up(ub_send.at[s, h], *up_sum(2 * s + 1, h, arrived))
                ub_copy(s, n).start()
                sent.append(ub_copy(s, n))

    def gate_step(s):
        xg_copy(s).wait_recv()
        if s > 0:
            ga_copy(s - 1).wait_recv()
        total = pg[2 * s, x] + xg_recv[2 * s].astype(F32)
        if s > 0:
            total = total + ga_recv[s - 1].astype(F32)
        ga_send[s] = total.astype(BF16)
        ga_copy(s).start()
        sent.append(ga_copy(s))
        if s < 3:
            if s > 0:
                gb_copy(s - 1).wait_recv()
            total = pg[2 * s + 1, x] + xg_recv[2 * s + 1].astype(F32)
            if s > 0:
                total = total + gb_recv[s - 1].astype(F32)
            gb_send[s] = total.astype(BF16)
            gb_copy(s).start()
            sent.append(gb_copy(s))

    up_pair(0)
    up_step(0)
    gate_pair(0)
    xg_copy(0).start()

    def pairs(s, carry):
        gate_pair(s)
        xg_copy(s).start()
        up_pair(s)
        return carry

    lax.fori_loop(1, 4, pairs, 0)
    gate_step(0)
    for s in range(1, 4):
        up_step(s)
        gate_step(s)

    xu_copy = remote(xu_send, xu_recv, xu_ss, xu_rs, xmate)
    for n in range(2):
        ua_copy(3, n).wait_recv()
        ub_copy(2, n).wait_recv()
        h = halves[n]
        body, squares = up_sum(7, h, [ua_recv.at[3, h], ub_recv.at[2, h]])
        if n == 0:
            put_up(xu_send, body, squares)
            xu_copy.start()
        else:
            pu[7, h, :, :HALF] = body
            pu[7, h, :, HALF:] = squares
    ga_copy(3).wait_recv()
    gb_copy(2).wait_recv()
    gate_sum = pg[7, x] + xg_recv[7].astype(F32) + ga_recv[3].astype(F32) + gb_recv[2].astype(F32)
    xu_copy.wait_recv()
    up_total, squares = up_sum(7, x, [xu_recv])
    scale = lax.rsqrt(squares[:, 0:1] / D + 1e-05)
    gate_sum = gate_sum * scale
    hidden = (gate_sum / (1.0 + jnp.exp(-gate_sum)) * (up_total * scale)).astype(BF16)
    h1[0, x] = hidden[:, :C1]
    h2[0, x] = hidden[:, C1:]

    def hidden_ref(kind, pos):
        return (h1.at[pos, x], h1.at[pos, x_other], h2.at[pos, x])[kind]

    def hz_copy(kind, pos, target, to):
        return remote(
            hidden_ref(kind, pos), hidden_ref(kind, target), hz_s.at[kind, target], hz_r.at[kind, target], to
        )

    def hx_copy(n, ref):
        return remote(ref, ref, hx_s.at[n], hx_r.at[n], xmate)

    def forward(kind, pos):
        if pos == 0:
            targets = ((1, ahead), (2, behind))
        elif pos % 2 == 1:
            targets = ((pos + 2, ahead),) if pos < 7 else ()
        else:
            targets = ((pos + 2, behind),) if pos < 6 else ()
        for target, to in targets:
            copy = hz_copy(kind, pos, target, to)
            copy.start()
            sent.append(copy)

    def to_xmate(pos):
        copy = hx_copy(pos, h2.at[pos, x])
        copy.start()
        sent.append(copy)

    def down_step(k):
        first, count = (0, 1) if k == 0 else (2 * k - 1, 2 if k < 4 else 1)
        for pos in range(first, first + count):
            hx_copy(pos, h2.at[pos, x_other]).wait_recv()
        left = h1[first : first + count].reshape(count * 64, C1)
        right = h2[first : first + count].reshape(count * 64, C2)
        for c in range(2):
            dp[k, c, : count * 64] = jnp.dot(
                left, down_w[c, :C1], preferred_element_type=F32
            ) + jnp.dot(right, down_w[c, C1:], preferred_element_type=F32)
        some = pl.ds(0, count * 64)
        copy = remote(
            dp.at[k, 1 - core, some], dr.at[k, some], dr_s.at[k], dr_r.at[k], mate
        )
        copy.start()
        sent.append(copy)

    def return_copy(pos, owner):
        return remote(ds_send.at[pos], fr.at[g], fr_s.at[pos], fr_r.at[g], (owner, b))

    returns = []

    def return_step(k):
        first, count = (0, 1) if k == 0 else (2 * k - 1, 2 if k < 4 else 1)
        some = pl.ds(0, count * 64)
        remote(dp.at[k, 1 - core, some], dr.at[k, some], dr_s.at[k], dr_r.at[k], mate).wait_recv()
        for j in range(count):
            pos = first + j
            there = count - 1 - j
            total = (
                dp[k, core, j * 64 : j * 64 + 64] + dr[k, there * 64 : there * 64 + 64]
            ).astype(BF16)
            ds_send[pos] = total
            owner = lax.rem(z + (-sign if j == 0 else sign) * k + RING, RING)
            returns.append((pos, owner))

            @pl.when(owner != g)
            def _():
                return_copy(pos, owner).start()

            @pl.when(owner == g)
            def _():
                fr[g] = total

    forward(2, 0)
    forward(0, 0)
    copy = hx_copy(8, h1.at[0, x])
    copy.start()
    sent.append(copy)
    to_xmate(0)
    pushes[3].wait()
    loads[2].wait()
    hx_copy(8, h1.at[0, x_other]).wait_recv()
    forward(1, 0)
    for k in range(1, 5):
        for kind in (2, 0, 1):
            for pos in (2 * k - 1, 2 * k) if k < 4 else (7,):
                hz_copy(kind, pos, pos, ahead).wait_recv()
                forward(kind, pos)
                if kind == 2:
                    to_xmate(pos)
        if k >= 2:
            return_step(k - 2)
        down_step(k - 1)
    return_step(3)
    down_step(4)
    return_step(4)

    total = wide_s[...]
    for n in ORDER:
        remote(
            ds_send.at[0], fr.at[source(n)], fr_s.at[0], fr_r.at[source(n)], (peer(n), b)
        ).wait_recv()
    for j in range(GROUPS):
        total = total + fr[j].astype(F32)
    out[...] = total

    for copy in merges + gathers + to_mate:
        copy.wait_send()
    for s in range(4):
        xg_copy(s).wait_send()
    xu_copy.wait_send()
    for copy in sent:
        copy.wait_send()
    for pos, owner in returns:

        @pl.when(owner != g)
        def _():
            return_copy(pos, owner).wait_send()


def feed_forward(w_in, st_in, res, gain, gate, up, down):
    vmem = pl.BlockSpec(memory_space=pltpu.VMEM)
    hbm = pl.BlockSpec(memory_space=pl.ANY)
    V = pltpu.VMEM
    dma = lambda *shape: pltpu.SemaphoreType.DMA(shape)
    scratch = [
        V((4, 64, FEAT), BF16), V((4, 64, 128), F32), V((64, FEAT), F32), V((2, 32, FEAT), BF16),
        V((2, 8, FEAT), F32),
        V((2 * FEAT, HALF), BF16), V((2 * FEAT, HALF), BF16), V((2, HALF, FEAT), BF16),
        V((8, 2, 32, 2 * FEAT), BF16), V((8, 2, 32, WIDE), F32), V((8, 2, 32, HALF), F32),
        V((8, 32, HALF), BF16), V((8, 32, HALF), BF16),
        V((4, 2, 32, WIDE), BF16), V((4, 2, 32, WIDE), BF16),
        V((3, 2, 32, WIDE), BF16), V((3, 2, 32, WIDE), BF16),
        V((4, 32, HALF), BF16), V((4, 32, HALF), BF16),
        V((3, 32, HALF), BF16), V((3, 32, HALF), BF16),
        V((32, WIDE), BF16), V((32, WIDE), BF16),
        V((8, 2, 32, C1), BF16), V((8, 2, 32, C2), BF16),
        V((5, 2, 128, FEAT), F32), V((5, 128, FEAT), F32),
        V((8, 64, FEAT), BF16), V((8, 64, FEAT), BF16),
        dma(3), dma(4), dma(4), dma(8), dma(8), dma(8), dma(8), dma(8), dma(8),
        dma(4), dma(4), dma(4, 2), dma(4, 2), dma(3, 2), dma(3, 2),
        dma(4), dma(4), dma(3), dma(3), pltpu.SemaphoreType.DMA, pltpu.SemaphoreType.DMA,
        dma(3, 8), dma(3, 8), dma(9), dma(9), dma(5), dma(5), dma(8), dma(8),
    ]
    return pl.pallas_call(
        kernel,
        out_shape=jax.ShapeDtypeStruct((64, FEAT), F32),
        in_specs=[vmem, vmem, vmem, vmem, hbm, hbm, hbm],
        out_specs=vmem,
        scratch_shapes=scratch,
        compiler_params=pltpu.CompilerParams(
            collective_id=0, has_side_effects=True, vmem_limit_bytes=50 * 1024 * 1024
        ),
        cost_estimate=pl.CostEstimate(
            flops=5_300_000_000, bytes_accessed=11_000_000, transcendentals=100_000
        ),
    )(w_in, st_in, res, gain, gate, up, down)


def on_device(
    residual_in,
    queries,
    key_cache,
    value_cache,
    key_new,
    value_new,
    lengths,
    ffn_gain,
    gate_weight,
    up_weight,
    down_weight,
):
    cycle_size = lax.axis_size("blk")
    quarters = cycle_size // KV_HEADS
    per_kv = HEADS // KV_HEADS
    own_heads = HEADS // cycle_size
    head_size = key_cache.shape[3]
    seq_rows = residual_in.shape[0]
    positions_here = key_cache.shape[2]
    blk_index = lax.axis_index("blk")
    kv_head = blk_index // quarters
    quarter = blk_index % quarters
    score_scale = 1.0 / math.sqrt(head_size)
    group_queries = lax.dynamic_slice_in_dim(
        queries, kv_head * per_kv * head_size, per_kv * head_size, 1
    )
    group_queries = group_queries.astype(F32).reshape(seq_rows, per_kv, head_size)
    fresh_key = lax.dynamic_slice_in_dim(key_new, kv_head * head_size, head_size, 1).astype(F32)
    fresh_value = lax.dynamic_slice_in_dim(value_new, kv_head * head_size, head_size, 1).astype(F32)
    keys_here = key_cache[:, 0].astype(F32)
    values_here = value_cache[:, 0].astype(F32)
    scores = jnp.einsum("shd,spd->shp", group_queries, keys_here) * score_scale
    fresh_scores = jnp.einsum("shd,sd->sh", group_queries, fresh_key) * score_scale
    places = quarter * positions_here + jnp.arange(positions_here, dtype=jnp.int32)
    usable = (places[None, :] < lengths[:, None])[:, None, :]
    with_fresh = quarter == 0
    largest = jnp.maximum(
        jnp.max(jnp.where(usable, scores, -1e30), axis=2),
        jnp.where(with_fresh, fresh_scores, -1e30),
    )
    weights = jnp.where(usable, jnp.exp(scores - largest[..., None]), 0.0)
    fresh_weight = jnp.where(with_fresh, jnp.exp(fresh_scores - largest), 0.0)
    totals = jnp.sum(weights, axis=2) + fresh_weight
    weighted = (
        jnp.einsum("shp,spd->shd", weights, values_here)
        + fresh_weight[..., None] * fresh_value[:, None, :]
    )
    w_in = weighted.astype(BF16).reshape(seq_rows, quarters, own_heads * head_size).transpose(1, 0, 2)
    stats = jnp.concatenate(
        [largest.reshape(seq_rows, quarters, own_heads), totals.reshape(seq_rows, quarters, own_heads)],
        axis=2,
    )
    st_in = jnp.pad(stats, ((0, 0), (0, 0), (0, 128 - 2 * own_heads))).transpose(1, 0, 2)
    return feed_forward(
        w_in, st_in, residual_in, ffn_gain.reshape(1, FEAT), gate_weight, up_weight, down_weight
    )


def solution(mesh):
    in_specs = (
        P("grp", "blk"),
        P("grp", None),
        P("grp", "blk", None, None),
        P("grp", "blk", None, None),
        P("grp", None),
        P("grp", None),
        P("grp"),
        P("blk"),
        P("blk", "grp"),
        P("blk", "grp"),
        P("grp", "blk"),
    )
    out_specs = P("grp", "blk")
    return jax.shard_map(
        on_device, mesh=mesh, in_specs=in_specs, out_specs=out_specs, check_vma=False
    )
```

```python
import functools
import math

import jax
import jax.numpy as jnp
from jax import lax
from jax.experimental import pallas as pl
from jax.experimental.pallas import tpu as pltpu
from jax.sharding import PartitionSpec as P

D = 16384
HEADS = 128
KV_HEADS = 8
MESH = pl.DeviceIdType.MESH
F32 = jnp.float32
BF16 = jnp.bfloat16

RING = 8
GROUPS = 8
FEAT = 512
HALF = 1664
WIDE = HALF + 128
C1 = 768
C2 = HALF - C1


def slot_of(distance):
    return jnp.where(distance <= 4, 8 - 2 * distance, 2 * distance - 9)


def kernel(
    queries, keys, values, key_new, value_new, lengths, res_in, gain_in, gate, up, down, out,
    q_s, k_s, v_s, kn_s, vn_s, len_s, res, gain, q32, kn32, vn32, att, stats_s, w_in, st_in, w_got, st_got, wide_s, token_s, inv_gain,
    gate_w, up_w, down_w, x_s, pu, pg,
    xg_send, xg_recv, ua_send, ua_recv, ub_send, ub_recv,
    ga_send, ga_recv, gb_send, gb_recv, xu_send, xu_recv,
    h1, h2, dp, dr, ds_send, fr,
    load_sem, local_sem, wsem_s, wsem_r, at_s, at_r, tok_s, tok_r, mate_s, mate_r,
    xg_ss, xg_rs, ua_ss, ua_rs, ub_ss, ub_rs, ga_ss, ga_rs, gb_ss, gb_rs, xu_ss, xu_rs,
    hz_s, hz_r, hx_s, hx_r, dr_s, dr_r, fr_s, fr_r,
):
    g = lax.axis_index("grp")
    b = lax.axis_index("blk")
    z = b // 4
    q = b % 4
    x = q // 2
    core = q % 2
    sign = 1 - 2 * core
    mate = (g, z * 4 + x * 2 + (1 - core))
    xmate = (g, z * 4 + (1 - x) * 2 + core)
    ahead = (g, lax.rem(z + sign + RING, RING) * 4 + q)
    behind = (g, lax.rem(z - sign + RING, RING) * 4 + q)
    x_other = 1 - x

    def remote(src, dst, ss, rs, to):
        return pltpu.make_async_remote_copy(
            src_ref=src, dst_ref=dst, send_sem=ss, recv_sem=rs, device_id=to, device_id_type=MESH
        )

    def peer(n):
        return (lax.rem(g // 4 + n // 4, 2)) * 4 + lax.rem(g % 4 + n % 4, 4)

    def source(n):
        return (lax.rem(g // 4 + n // 4, 2)) * 4 + lax.rem(g % 4 - n % 4 + 4, 4)

    ORDER = (1, 3, 2, 4, 5, 7, 6)

    mine = pl.ds(pl.multiple_of(core * HALF, 128), HALF)
    other = pl.ds(pl.multiple_of((1 - core) * HALF, 128), HALF)
    rows = pl.ds(pl.multiple_of(core * FEAT, FEAT), FEAT)
    head_lanes = pl.ds(pl.multiple_of(z * 128, 128), 128)
    cache_loads = [
        pltpu.make_async_copy(
            queries.at[:, pl.ds(pl.multiple_of(z * 2048, 2048), 2048)], q_s, load_sem.at[0]
        ),
        pltpu.make_async_copy(key_new.at[:, head_lanes], kn_s, load_sem.at[1]),
        pltpu.make_async_copy(value_new.at[:, head_lanes], vn_s, load_sem.at[2]),
        pltpu.make_async_copy(lengths, len_s, load_sem.at[5]),
        pltpu.make_async_copy(keys.at[:, 0], k_s, load_sem.at[3]),
        pltpu.make_async_copy(values.at[:, 0], v_s, load_sem.at[4]),
        pltpu.make_async_copy(res_in, res, load_sem.at[6]),
        pltpu.make_async_copy(gain_in, gain, load_sem.at[7]),
    ]
    for load in cache_loads:
        load.start()
    loads = [
        pltpu.make_async_copy(gate.at[:, mine], gate_w.at[rows], local_sem.at[0]),
        pltpu.make_async_copy(up.at[:, mine], up_w.at[rows], local_sem.at[1]),
        pltpu.make_async_copy(down.at[mine], down_w.at[core], local_sem.at[2]),
    ]
    st_got[...] = jnp.zeros((128, 128), F32)
    barrier = pltpu.get_barrier_semaphore()
    partners = [mate, xmate, (g, z * 4 + (1 - x) * 2 + (1 - core)), ahead, behind]
    partners += [(peer(n), b) for n in ORDER]
    for partner in partners:
        pl.semaphore_signal(barrier, inc=1, device_id=partner, device_id_type=MESH)

    pl.semaphore_wait(barrier, len(partners))

    pushes = [
        remote(inv_gain.at[core], inv_gain.at[core], wsem_s.at[0], wsem_r.at[0], mate),
        remote(up.at[:, other], up_w.at[rows], wsem_s.at[1], wsem_r.at[1], mate),
        remote(gate.at[:, other], gate_w.at[rows], wsem_s.at[2], wsem_r.at[2], mate),
        remote(down.at[other], down_w.at[core], wsem_s.at[3], wsem_r.at[3], mate),
    ]
    for load in cache_loads:
        load.wait()
    for load in loads[:2]:
        load.start()
    gain_row = gain[...].astype(F32).reshape(1, FEAT)
    inv_gain[core] = jnp.broadcast_to(1.0 / gain_row, (8, FEAT))
    for push in pushes[:3]:
        push.start()
    loads[2].start()
    q32[...] = q_s[...].astype(F32)
    kn32[...] = kn_s[...].astype(F32)
    vn32[...] = vn_s[...].astype(F32)
    score_scale = 1.0 / math.sqrt(128)
    lane8 = lax.broadcasted_iota(jnp.int32, (8, 128), 1)
    row8 = lax.broadcasted_iota(jnp.int32, (8, 128), 0)
    row = lax.broadcasted_iota(jnp.int32, (128, 512), 0)
    col = lax.broadcasted_iota(jnp.int32, (128, 512), 1)
    same = lax.rem(row, 8) == col // 64
    place = q * 64 + lax.rem(col, 64)

    def attend(i, carry):
        eight = pl.ds(pl.multiple_of(i * 8, 8), 8)
        q8 = q32[eight]
        q_rows = jnp.concatenate([q8[:, h * 128 : h * 128 + 128] for h in range(16)], axis=0)
        k_rows = k_s[eight].reshape(512, 128)
        v_rows = v_s[eight].reshape(512, 128)
        spread = lambda a: jnp.concatenate([a] * 16, axis=0)
        limit = jnp.zeros((8, 128), jnp.int32)
        for n in range(8):
            limit = jnp.where(row8 == n, len_s[i * 8 + n], limit)
        usable = same & (place < spread(limit)[:, 0:1])
        scores = lax.dot_general(
            q_rows.astype(BF16), k_rows, (((1,), (1,)), ((), ())), preferred_element_type=F32
        )
        scores = jnp.where(usable, scores * score_scale, -1e30)
        fresh = jnp.sum(q_rows * spread(kn32[eight]), axis=1, keepdims=True) * score_scale
        fresh = jnp.where(q == 0, fresh, -1e30)
        top = jnp.maximum(jnp.max(scores, axis=1, keepdims=True), fresh)
        weights = jnp.where(usable, jnp.exp(scores - top), 0.0)
        fresh_weight = jnp.where(q == 0, jnp.exp(fresh - top), 0.0)
        total = jnp.sum(weights, axis=1, keepdims=True) + fresh_weight
        mixed = jnp.dot(weights.astype(BF16), v_rows, preferred_element_type=F32)
        mixed = mixed + fresh_weight * spread(vn32[eight])
        att[:, eight] = mixed.reshape(16, 8, 128)
        stats = jnp.zeros((8, 128), F32)
        for h in range(16):
            at = h // 4 * 8 + h % 4
            stats = jnp.where(lane8 == at, top[h * 8 : h * 8 + 8], stats)
            stats = jnp.where(lane8 == at + 4, total[h * 8 : h * 8 + 8], stats)
        stats_s[eight] = stats
        return carry

    stats_s[64:] = jnp.zeros((64, 128), F32)
    lax.fori_loop(0, 8, attend, 0, unroll=8)
    st_in[...] = jnp.transpose(stats_s[...])[:32]
    w_in[...] = att[...].astype(BF16).reshape(4, 4, 64, 128)

    eight_of = lambda n: pl.ds(pl.multiple_of(n * 8, 8), 8)
    merges = []
    for n in (3, 2, 1):
        p = q ^ n
        to = (g, z * 4 + p)
        merges.append(remote(st_in.at[eight_of(p)], st_got.at[eight_of(q)], at_s.at[n], at_r.at[q], to))
        merges.append(remote(w_in.at[p], w_got.at[q], at_s.at[4 + n], at_r.at[4 + q], to))
    for copy in merges:
        copy.start()
    st_got[eight_of(q)] = st_in[eight_of(q)]
    w_got[q] = w_in[q]
    for n in (1, 2, 3):
        p = q ^ n
        to = (g, z * 4 + p)
        remote(
            st_in.at[eight_of(p)], st_got.at[eight_of(p)], at_s.at[n], at_r.at[p], to
        ).wait_recv()
        remote(w_in.at[p], w_got.at[p], at_s.at[4 + n], at_r.at[4 + p], to).wait_recv()
    got = jnp.transpose(st_got[...])[:64]
    for head in range(4):
        cols = slice(head * 128, head * 128 + 128)
        tops = [got[:, j * 8 + head : j * 8 + head + 1] for j in range(4)]
        sums = [got[:, j * 8 + head + 4 : j * 8 + head + 5] for j in range(4)]
        top = jnp.maximum(jnp.maximum(tops[0], tops[1]), jnp.maximum(tops[2], tops[3]))
        factors = [jnp.exp(t - top) for t in tops]
        total = sum(f * s for f, s in zip(factors, sums))
        mixed = sum(f * w_got[j, head].astype(F32) for j, f in enumerate(factors))
        wide = res[:, cols].astype(F32) + mixed / total
        wide_s[:, cols] = wide
        scaled = (wide * gain_row[:, cols]).astype(BF16)
        token_s[0, :, cols] = scaled[:32]
        token_s[1, :, cols] = scaled[32:]

    def slots(owner):
        away = lax.rem((owner - z) * sign + 2 * RING - 1, RING) + 1
        back = lax.rem(RING - away + RING - 1, RING) + 1
        return slot_of(away), slot_of(back)

    lanes = pl.ds(pl.multiple_of(core * FEAT, FEAT), FEAT)
    own_slot, own_mate_slot = slots(g)
    gathers = []
    for n in ORDER[::-1]:
        gathers.append(
            remote(token_s, x_s.at[own_slot, :, :, lanes], tok_s.at[n], tok_r.at[n], (peer(n), b))
        )
    for copy in gathers:
        copy.start()
    x_s[own_slot, :, :, lanes] = token_s[...]
    to_mate = [remote(token_s, x_s.at[own_mate_slot, :, :, lanes], mate_s.at[0], mate_r.at[0], mate)]
    to_mate[0].start()
    for n in ORDER:
        here, there = slots(source(n))
        remote(
            token_s, x_s.at[here, :, :, lanes], tok_s.at[n], tok_r.at[n], (peer(n), b)
        ).wait_recv()
        copy = remote(
            x_s.at[here, :, :, lanes], x_s.at[there, :, :, lanes], mate_s.at[n], mate_r.at[n], mate
        )
        copy.start()
        to_mate.append(copy)
    for load in loads[:2]:
        load.wait()
    for push in pushes[:3]:
        push.wait()

    other_rows = pl.ds(pl.multiple_of((1 - core) * FEAT, FEAT), FEAT)

    def up_first(lanes_of, add):
        tokens = x_s[pl.ds(0, 2), :, :, lanes_of].reshape(128, FEAT)
        for lo in range(0, HALF, 512):
            hi = min(lo + 512, HALF)
            part = jnp.dot(tokens, up_w[lanes_of, lo:hi], preferred_element_type=F32)
            part = part.reshape(2, 2, 32, hi - lo)
            pu[0:2, :, :, lo:hi] = pu[0:2, :, :, lo:hi] + part if add else part

    up_first(rows, False)
    for copy in to_mate:
        copy.wait_recv()
    pushes[3].start()
    up_first(other_rows, True)

    lane = lax.broadcasted_iota(jnp.int32, (32, 128), 1)

    def project(s):
        tokens = x_s[pl.ds(s * 2, 2)].reshape(128, 2 * FEAT)
        return tokens

    def up_pair(s):
        tokens = project(s)
        for lo in range(0, HALF, 512):
            hi = min(lo + 512, HALF)
            part = jnp.dot(tokens, up_w[:, lo:hi], preferred_element_type=F32)
            pu[pl.ds(s * 2, 2), :, :, lo:hi] = part.reshape(2, 2, 32, hi - lo)
        square_sums(s)

    def square_sums(s):
        tokens = project(s)
        plain = [
            tokens[:, c * FEAT : (c + 1) * FEAT].astype(F32) * inv_gain[c, 0:1] for c in range(2)
        ]
        squares = plain[0] * plain[0] + plain[1] * plain[1]
        total = jnp.sum(squares, axis=1, keepdims=True)
        pu[pl.ds(s * 2, 2), :, :, HALF:] = jnp.broadcast_to(total, (128, 128)).reshape(2, 2, 32, 128)

    def gate_pair(s):
        tokens = project(s)
        for lo in range(0, HALF, 512):
            hi = min(lo + 512, HALF)
            part = jnp.dot(tokens, gate_w[:, lo:hi], preferred_element_type=F32)
            pg[pl.ds(s * 2, 2), :, :, lo:hi] = part.reshape(2, 2, 32, hi - lo)
        xg_send[pl.ds(s * 2, 2)] = pg[pl.ds(s * 2, 2), x_other].astype(BF16)

    def xg_copy(n):
        return remote(xg_send.at[n], xg_recv.at[n], xg_ss.at[n], xg_rs.at[n], xmate)

    def up_sum(block, half, arrived):
        body = pu[block, half, :, :HALF]
        squares = pu[block, half, :, HALF:]
        for ref in arrived:
            body = body + ref[:, :HALF].astype(F32)
            halves = ref[:, HALF:].astype(F32)
            squares = squares + halves + pltpu.roll(halves, 64, 1)
        return body, squares

    def put_up(ref, body, squares):
        ref[:, :HALF] = body.astype(BF16)
        high = squares.astype(BF16)
        low = (squares - high.astype(F32)).astype(BF16)
        ref[:, HALF:] = jnp.where(lane < 64, high.astype(F32), low.astype(F32)).astype(BF16)

    halves = (x_other, x)
    sent = []

    def ua_copy(s, n):
        h = halves[n]
        return remote(ua_send.at[s, h], ua_recv.at[s, h], ua_ss.at[s, n], ua_rs.at[s, n], ahead)

    def ub_copy(s, n):
        h = halves[n]
        return remote(ub_send.at[s, h], ub_recv.at[s, h], ub_ss.at[s, n], ub_rs.at[s, n], behind)

    def ga_copy(s):
        return remote(ga_send.at[s], ga_recv.at[s], ga_ss.at[s], ga_rs.at[s], ahead)

    def gb_copy(s):
        return remote(gb_send.at[s], gb_recv.at[s], gb_ss.at[s], gb_rs.at[s], behind)

    def up_step(s):
        for n in range(2):
            h = halves[n]
            if s > 0:
                ua_copy(s - 1, n).wait_recv()
            arrived = [ua_recv.at[s - 1, h]] if s > 0 else []
            put_up(ua_send.at[s, h], *up_sum(2 * s, h, arrived))
            ua_copy(s, n).start()
            sent.append(ua_copy(s, n))
            if s < 3:
                if s > 0:
                    ub_copy(s - 1, n).wait_recv()
                arrived = [ub_recv.at[s - 1, h]] if s > 0 else []
                put_up(ub_send.at[s, h], *up_sum(2 * s + 1, h, arrived))
                ub_copy(s, n).start()
                sent.append(ub_copy(s, n))

    def gate_step(s):
        xg_copy(2 * s).wait_recv()
        if s > 0:
            ga_copy(s - 1).wait_recv()
        total = pg[2 * s, x] + xg_recv[2 * s].astype(F32)
        if s > 0:
            total = total + ga_recv[s - 1].astype(F32)
        ga_send[s] = total.astype(BF16)
        ga_copy(s).start()
        sent.append(ga_copy(s))
        if s < 3:
            xg_copy(2 * s + 1).wait_recv()
            if s > 0:
                gb_copy(s - 1).wait_recv()
            total = pg[2 * s + 1, x] + xg_recv[2 * s + 1].astype(F32)
            if s > 0:
                total = total + gb_recv[s - 1].astype(F32)
            gb_send[s] = total.astype(BF16)
            gb_copy(s).start()
            sent.append(gb_copy(s))

    square_sums(0)
    up_step(0)
    gate_pair(0)
    xg_copy(0).start()
    xg_copy(1).start()

    def pairs(s, carry):
        gate_pair(s)
        xg_copy(2 * s).start()
        xg_copy(2 * s + 1).start()
        up_pair(s)
        return carry

    lax.fori_loop(1, 4, pairs, 0)
    gate_step(0)
    for s in range(1, 4):
        up_step(s)
        gate_step(s)

    xu_copy = remote(xu_send, xu_recv, xu_ss, xu_rs, xmate)
    for n in range(2):
        ua_copy(3, n).wait_recv()
        ub_copy(2, n).wait_recv()
        h = halves[n]
        body, squares = up_sum(7, h, [ua_recv.at[3, h], ub_recv.at[2, h]])
        if n == 0:
            put_up(xu_send, body, squares)
            xu_copy.start()
        else:
            pu[7, h, :, :HALF] = body
            pu[7, h, :, HALF:] = squares
    xg_copy(7).wait_recv()
    ga_copy(3).wait_recv()
    gb_copy(2).wait_recv()
    gate_sum = pg[7, x] + xg_recv[7].astype(F32) + ga_recv[3].astype(F32) + gb_recv[2].astype(F32)
    xu_copy.wait_recv()
    up_total, squares = up_sum(7, x, [xu_recv])
    scale = lax.rsqrt(squares[:, 0:1] / D + 1e-05)
    gate_sum = gate_sum * scale
    hidden = (gate_sum / (1.0 + jnp.exp(-gate_sum)) * (up_total * scale)).astype(BF16)
    h1[0, x] = hidden[:, :C1]
    h2[0, x] = hidden[:, C1:]

    def hidden_ref(kind, pos):
        return (h1.at[pos, x], h1.at[pos, x_other], h2.at[pos, x])[kind]

    def hz_copy(kind, pos, target, to):
        return remote(
            hidden_ref(kind, pos), hidden_ref(kind, target), hz_s.at[kind, target], hz_r.at[kind, target], to
        )

    def hx_copy(n, ref):
        return remote(ref, ref, hx_s.at[n], hx_r.at[n], xmate)

    def forward(kind, pos):
        if pos == 0:
            targets = ((1, ahead), (2, behind))
        elif pos % 2 == 1:
            targets = ((pos + 2, ahead),) if pos < 7 else ()
        else:
            targets = ((pos + 2, behind),) if pos < 6 else ()
        for target, to in targets:
            copy = hz_copy(kind, pos, target, to)
            copy.start()
            sent.append(copy)

    def to_xmate(pos):
        copy = hx_copy(pos, h2.at[pos, x])
        copy.start()
        sent.append(copy)

    def step_blocks(k):
        return (0, 1) if k == 0 else (2 * k - 1, 2 if k < 4 else 1)

    def mate_sums(k):
        some = pl.ds(0, step_blocks(k)[1] * 64)
        return remote(dp.at[k, 1 - core, some], dr.at[k, some], dr_s.at[k], dr_r.at[k], mate)

    def down_parts(k):
        first, count = step_blocks(k)

        def part(n):
            if n == 0:
                for pos in range(first, first + count):
                    hx_copy(pos, h2.at[pos, x_other]).wait_recv()
            c, cols = n // 2, slice(n % 2 * 256, n % 2 * 256 + 256)
            left = h1[first : first + count].reshape(count * 64, C1)
            right = h2[first : first + count].reshape(count * 64, C2)
            dp[k, c, : count * 64, cols] = jnp.dot(
                left, down_w[c, :C1, cols], preferred_element_type=F32
            ) + jnp.dot(right, down_w[c, C1:, cols], preferred_element_type=F32)
            if n == 3:
                mate_sums(k).start()
                sent.append(mate_sums(k))

        return [functools.partial(part, n) for n in range(4)]

    def return_copy(pos, owner):
        return remote(ds_send.at[pos], fr.at[g], fr_s.at[pos], fr_r.at[g], (owner, b))

    returns = []

    def return_parts(k):
        first, count = step_blocks(k)

        def part(j):
            if j == 0:
                mate_sums(k).wait_recv()
            pos = first + j
            there = count - 1 - j
            total = (
                dp[k, core, j * 64 : j * 64 + 64] + dr[k, there * 64 : there * 64 + 64]
            ).astype(BF16)
            ds_send[pos] = total
            owner = lax.rem(z + (-sign if j == 0 else sign) * k + RING, RING)
            returns.append((pos, owner))

            @pl.when(owner != g)
            def _():
                return_copy(pos, owner).start()

            @pl.when(owner == g)
            def _():
                fr[g] = total

        return [functools.partial(part, j) for j in range(count)]

    forward(2, 0)
    forward(0, 0)
    copy = hx_copy(8, h1.at[0, x])
    copy.start()
    sent.append(copy)
    to_xmate(0)
    pushes[3].wait()
    loads[2].wait()
    hx_copy(8, h1.at[0, x_other]).wait_recv()
    forward(1, 0)
    for k in range(1, 5):
        parts = down_parts(k - 1)
        if k >= 2:
            parts = return_parts(k - 2) + parts
        arrivals = [(kind, pos) for kind in (2, 0, 1) for pos in ((2 * k - 1, 2 * k) if k < 4 else (7,))]
        for n, (kind, pos) in enumerate(arrivals):
            hz_copy(kind, pos, pos, ahead).wait_recv()
            forward(kind, pos)
            if kind == 2:
                to_xmate(pos)
            due = (n + 1) * len(parts) // len(arrivals) - n * len(parts) // len(arrivals)
            for part in parts[n * len(parts) // len(arrivals) :][:due]:
                part()
    for part in return_parts(3) + down_parts(4) + return_parts(4):
        part()

    total = wide_s[...]
    for n in ORDER:
        remote(
            ds_send.at[0], fr.at[source(n)], fr_s.at[0], fr_r.at[source(n)], (peer(n), b)
        ).wait_recv()
    for j in range(GROUPS):
        total = total + fr[j].astype(F32)
    out[...] = total

    for copy in merges + gathers + to_mate:
        copy.wait_send()
    for n in range(8):
        xg_copy(n).wait_send()
    xu_copy.wait_send()
    for copy in sent:
        copy.wait_send()
    for pos, owner in returns:

        @pl.when(owner != g)
        def _():
            return_copy(pos, owner).wait_send()


def layer(queries, keys, values, key_new, value_new, lengths, res, gain, gate, up, down):
    vmem = pl.BlockSpec(memory_space=pltpu.VMEM)
    hbm = pl.BlockSpec(memory_space=pl.ANY)
    V = pltpu.VMEM
    dma = lambda *shape: pltpu.SemaphoreType.DMA(shape)
    scratch = [
        V((64, 2048), BF16), V((64, 64, 128), BF16), V((64, 64, 128), BF16),
        V((64, 128), BF16), V((64, 128), BF16), pltpu.SMEM((64,), jnp.int32),
        V((64, FEAT), BF16), V((FEAT,), BF16),
        V((64, 2048), F32), V((64, 128), F32), V((64, 128), F32), V((16, 64, 128), F32),
        V((128, 128), F32), V((4, 4, 64, 128), BF16), V((32, 128), F32),
        V((4, 4, 64, 128), BF16), V((128, 128), F32), V((64, FEAT), F32), V((2, 32, FEAT), BF16),
        V((2, 8, FEAT), F32),
        V((2 * FEAT, HALF), BF16), V((2 * FEAT, HALF), BF16), V((2, HALF, FEAT), BF16),
        V((8, 2, 32, 2 * FEAT), BF16), V((8, 2, 32, WIDE), F32), V((8, 2, 32, HALF), F32),
        V((8, 32, HALF), BF16), V((8, 32, HALF), BF16),
        V((4, 2, 32, WIDE), BF16), V((4, 2, 32, WIDE), BF16),
        V((3, 2, 32, WIDE), BF16), V((3, 2, 32, WIDE), BF16),
        V((4, 32, HALF), BF16), V((4, 32, HALF), BF16),
        V((3, 32, HALF), BF16), V((3, 32, HALF), BF16),
        V((32, WIDE), BF16), V((32, WIDE), BF16),
        V((8, 2, 32, C1), BF16), V((8, 2, 32, C2), BF16),
        V((5, 2, 128, FEAT), F32), V((5, 128, FEAT), F32),
        V((8, 64, FEAT), BF16), V((8, 64, FEAT), BF16),
        dma(8), dma(3), dma(4), dma(4), dma(8), dma(8), dma(8), dma(8), dma(8), dma(8),
        dma(8), dma(8), dma(4, 2), dma(4, 2), dma(3, 2), dma(3, 2),
        dma(4), dma(4), dma(3), dma(3), pltpu.SemaphoreType.DMA, pltpu.SemaphoreType.DMA,
        dma(3, 8), dma(3, 8), dma(9), dma(9), dma(5), dma(5), dma(8), dma(8),
    ]
    return pl.pallas_call(
        kernel,
        out_shape=pltpu.VMEM((64, FEAT), F32),
        in_specs=[hbm] * 11,
        out_specs=vmem,
        scratch_shapes=scratch,
        compiler_params=pltpu.CompilerParams(
            collective_id=0, has_side_effects=True, vmem_limit_bytes=61 * 1024 * 1024
        ),
        cost_estimate=pl.CostEstimate(
            flops=5_300_000_000, bytes_accessed=11_000_000, transcendentals=100_000
        ),
    )(queries, keys, values, key_new, value_new, lengths, res, gain, gate, up, down)


def on_device(
    residual_in,
    queries,
    key_cache,
    value_cache,
    key_new,
    value_new,
    lengths,
    ffn_gain,
    gate_weight,
    up_weight,
    down_weight,
):
    return layer(
        queries,
        key_cache,
        value_cache,
        key_new,
        value_new,
        lengths,
        residual_in,
        ffn_gain,
        gate_weight,
        up_weight,
        down_weight,
    )


def solution(mesh):
    in_specs = (
        P("grp", "blk"),
        P("grp", None),
        P("grp", "blk", None, None),
        P("grp", "blk", None, None),
        P("grp", None),
        P("grp", None),
        P("grp"),
        P("blk"),
        P("blk", "grp"),
        P("blk", "grp"),
        P("grp", "blk"),
    )
    out_specs = P("grp", "blk")
    return jax.shard_map(
        on_device, mesh=mesh, in_specs=in_specs, out_specs=out_specs, check_vma=False
    )
```

```python
import functools
import math

import jax
import jax.numpy as jnp
from jax import lax
from jax.experimental import pallas as pl
from jax.experimental.pallas import tpu as pltpu
from jax.sharding import PartitionSpec as P

D = 16384
HEADS = 128
KV_HEADS = 8
MESH = pl.DeviceIdType.MESH
F32 = jnp.float32
BF16 = jnp.bfloat16

RING = 8
GROUPS = 8
FEAT = 512
HALF = 1664
TAIL = 384
UP = HALF - TAIL
WIDE = UP + 128
GATE = HALF + TAIL
C1 = 768
C2 = HALF - C1


def slot_of(distance):
    return jnp.where(distance <= 4, 8 - 2 * distance, 2 * distance - 9)


def kernel(
    queries, keys, values, key_new, value_new, lengths, res_in, gain_in, gate, up, down, out,
    q_s, k_s, v_s, kn_s, vn_s, len_s, res, gain, q32, kn32, vn32, att, stats_s, w_in, st_in, w_got, st_got, wide_s, token_s, inv_gain,
    gate_w, up_w, down_w, x_s, pu, pg,
    xg_send, xg_recv, ua_send, ua_recv, ub_send, ub_recv,
    ga_send, ga_recv, gb_send, gb_recv, xu_send, xu_recv,
    h1, h2, dp, dr, ds_send, fr,
    load_sem, local_sem, wsem_s, wsem_r, at_s, at_r, tok_s, tok_r, mate_s, mate_r,
    xg_ss, xg_rs, ua_ss, ua_rs, ub_ss, ub_rs, ga_ss, ga_rs, gb_ss, gb_rs, xu_ss, xu_rs,
    hz_s, hz_r, hx_s, hx_r, dr_s, dr_r, fr_s, fr_r,
):
    g = lax.axis_index("grp")
    b = lax.axis_index("blk")
    z = b // 4
    q = b % 4
    x = q // 2
    core = q % 2
    sign = 1 - 2 * core
    mate = (g, z * 4 + x * 2 + (1 - core))
    xmate = (g, z * 4 + (1 - x) * 2 + core)
    ahead = (g, lax.rem(z + sign + RING, RING) * 4 + q)
    behind = (g, lax.rem(z - sign + RING, RING) * 4 + q)
    x_other = 1 - x

    def remote(src, dst, ss, rs, to):
        return pltpu.make_async_remote_copy(
            src_ref=src, dst_ref=dst, send_sem=ss, recv_sem=rs, device_id=to, device_id_type=MESH
        )

    def peer(n):
        return (lax.rem(g // 4 + n // 4, 2)) * 4 + lax.rem(g % 4 + n % 4, 4)

    def source(n):
        return (lax.rem(g // 4 + n // 4, 2)) * 4 + lax.rem(g % 4 - n % 4 + 4, 4)

    ORDER = (1, 3, 2, 4, 5, 7, 6)
    FAR_FIRST = (6, 5, 7, 4, 2, 1, 3)

    mine = pl.ds(pl.multiple_of(core * HALF, 128), HALF)
    other = pl.ds(pl.multiple_of((1 - core) * HALF, 128), HALF)
    rows = pl.ds(pl.multiple_of(core * FEAT, FEAT), FEAT)
    head_lanes = pl.ds(pl.multiple_of(z * 128, 128), 128)
    cache_loads = [
        pltpu.make_async_copy(
            queries.at[:, pl.ds(pl.multiple_of(z * 2048, 2048), 2048)], q_s, load_sem.at[0]
        ),
        pltpu.make_async_copy(key_new.at[:, head_lanes], kn_s, load_sem.at[1]),
        pltpu.make_async_copy(value_new.at[:, head_lanes], vn_s, load_sem.at[2]),
        pltpu.make_async_copy(lengths, len_s, load_sem.at[5]),
        pltpu.make_async_copy(keys.at[:, 0], k_s, load_sem.at[3]),
        pltpu.make_async_copy(values.at[:, 0], v_s, load_sem.at[4]),
        pltpu.make_async_copy(res_in, res, load_sem.at[6]),
        pltpu.make_async_copy(gain_in, gain, load_sem.at[7]),
    ]
    for load in cache_loads:
        load.start()
    loads = [
        pltpu.make_async_copy(gate.at[:, mine], gate_w.at[rows], local_sem.at[0]),
        pltpu.make_async_copy(up.at[:, mine], up_w.at[rows], local_sem.at[1]),
        pltpu.make_async_copy(down.at[mine], down_w.at[core], local_sem.at[2]),
    ]
    st_got[...] = jnp.zeros((128, 128), F32)
    barrier = pltpu.get_barrier_semaphore()
    partners = [mate, xmate, (g, z * 4 + (1 - x) * 2 + (1 - core)), ahead, behind]
    partners += [(peer(n), b) for n in ORDER]
    for partner in partners:
        pl.semaphore_signal(barrier, inc=1, device_id=partner, device_id_type=MESH)

    pl.semaphore_wait(barrier, len(partners))

    pushes = [
        remote(inv_gain.at[core], inv_gain.at[core], wsem_s.at[0], wsem_r.at[0], mate),
        remote(up.at[:, other], up_w.at[rows], wsem_s.at[1], wsem_r.at[1], mate),
        remote(gate.at[:, other], gate_w.at[rows], wsem_s.at[2], wsem_r.at[2], mate),
        remote(down.at[other], down_w.at[core], wsem_s.at[3], wsem_r.at[3], mate),
    ]
    for load in cache_loads:
        load.wait()
    for load in loads[:2]:
        load.start()
    gain_row = gain[...].astype(F32).reshape(1, FEAT)
    inv_gain[core] = jnp.broadcast_to(1.0 / gain_row, (8, FEAT))
    for push in pushes[:3]:
        push.start()
    loads[2].start()
    q32[...] = q_s[...].astype(F32)
    kn32[...] = kn_s[...].astype(F32)
    vn32[...] = vn_s[...].astype(F32)
    score_scale = 1.0 / math.sqrt(128)
    lane8 = lax.broadcasted_iota(jnp.int32, (8, 128), 1)
    row8 = lax.broadcasted_iota(jnp.int32, (8, 128), 0)
    row = lax.broadcasted_iota(jnp.int32, (128, 512), 0)
    col = lax.broadcasted_iota(jnp.int32, (128, 512), 1)
    same = lax.rem(row, 8) == col // 64
    place = q * 64 + lax.rem(col, 64)

    def attend(i, carry):
        eight = pl.ds(pl.multiple_of(i * 8, 8), 8)
        q8 = q32[eight]
        q_rows = jnp.concatenate([q8[:, h * 128 : h * 128 + 128] for h in range(16)], axis=0)
        k_rows = k_s[eight].reshape(512, 128)
        v_rows = v_s[eight].reshape(512, 128)
        spread = lambda a: jnp.concatenate([a] * 16, axis=0)
        limit = jnp.zeros((8, 128), jnp.int32)
        for n in range(8):
            limit = jnp.where(row8 == n, len_s[i * 8 + n], limit)
        usable = same & (place < spread(limit)[:, 0:1])
        scores = lax.dot_general(
            q_rows.astype(BF16), k_rows, (((1,), (1,)), ((), ())), preferred_element_type=F32
        )
        scores = jnp.where(usable, scores * score_scale, -1e30)
        fresh = jnp.sum(q_rows * spread(kn32[eight]), axis=1, keepdims=True) * score_scale
        fresh = jnp.where(q == 0, fresh, -1e30)
        top = jnp.maximum(jnp.max(scores, axis=1, keepdims=True), fresh)
        weights = jnp.where(usable, jnp.exp(scores - top), 0.0)
        fresh_weight = jnp.where(q == 0, jnp.exp(fresh - top), 0.0)
        total = jnp.sum(weights, axis=1, keepdims=True) + fresh_weight
        mixed = jnp.dot(weights.astype(BF16), v_rows, preferred_element_type=F32)
        mixed = mixed + fresh_weight * spread(vn32[eight])
        att[:, eight] = mixed.reshape(16, 8, 128)
        stats = jnp.zeros((8, 128), F32)
        for h in range(16):
            at = h // 4 * 8 + h % 4
            stats = jnp.where(lane8 == at, top[h * 8 : h * 8 + 8], stats)
            stats = jnp.where(lane8 == at + 4, total[h * 8 : h * 8 + 8], stats)
        stats_s[eight] = stats
        return carry

    stats_s[64:] = jnp.zeros((64, 128), F32)
    lax.fori_loop(0, 8, attend, 0, unroll=8)
    st_in[...] = jnp.transpose(stats_s[...])[:32]
    w_in[...] = att[...].astype(BF16).reshape(4, 4, 64, 128)

    eight_of = lambda n: pl.ds(pl.multiple_of(n * 8, 8), 8)
    merges = []
    for n in (3, 2, 1):
        p = q ^ n
        to = (g, z * 4 + p)
        merges.append(remote(st_in.at[eight_of(p)], st_got.at[eight_of(q)], at_s.at[n], at_r.at[q], to))
        merges.append(remote(w_in.at[p], w_got.at[q], at_s.at[4 + n], at_r.at[4 + q], to))
    for copy in merges:
        copy.start()
    st_got[eight_of(q)] = st_in[eight_of(q)]
    w_got[q] = w_in[q]
    for n in (1, 2, 3):
        p = q ^ n
        to = (g, z * 4 + p)
        remote(
            st_in.at[eight_of(p)], st_got.at[eight_of(p)], at_s.at[n], at_r.at[p], to
        ).wait_recv()
        remote(w_in.at[p], w_got.at[p], at_s.at[4 + n], at_r.at[4 + p], to).wait_recv()
    got = jnp.transpose(st_got[...])[:64]
    for head in range(4):
        cols = slice(head * 128, head * 128 + 128)
        tops = [got[:, j * 8 + head : j * 8 + head + 1] for j in range(4)]
        sums = [got[:, j * 8 + head + 4 : j * 8 + head + 5] for j in range(4)]
        top = jnp.maximum(jnp.maximum(tops[0], tops[1]), jnp.maximum(tops[2], tops[3]))
        factors = [jnp.exp(t - top) for t in tops]
        total = sum(f * s for f, s in zip(factors, sums))
        mixed = sum(f * w_got[j, head].astype(F32) for j, f in enumerate(factors))
        wide = res[:, cols].astype(F32) + mixed / total
        wide_s[:, cols] = wide
        scaled = (wide * gain_row[:, cols]).astype(BF16)
        token_s[0, :, cols] = scaled[:32]
        token_s[1, :, cols] = scaled[32:]

    def slots(owner):
        away = lax.rem((owner - z) * sign + 2 * RING - 1, RING) + 1
        back = lax.rem(RING - away + RING - 1, RING) + 1
        return slot_of(away), slot_of(back)

    lanes = pl.ds(pl.multiple_of(core * FEAT, FEAT), FEAT)
    own_slot, own_mate_slot = slots(g)
    gathers = []
    for n in FAR_FIRST:
        gathers.append(
            remote(token_s, x_s.at[own_slot, :, :, lanes], tok_s.at[n], tok_r.at[n], (peer(n), b))
        )
    for copy in gathers:
        copy.start()
    x_s[own_slot, :, :, lanes] = token_s[...]
    to_mate = [remote(token_s, x_s.at[own_mate_slot, :, :, lanes], mate_s.at[0], mate_r.at[0], mate)]
    to_mate[0].start()
    for n in FAR_FIRST:
        here, there = slots(source(n))
        remote(
            token_s, x_s.at[here, :, :, lanes], tok_s.at[n], tok_r.at[n], (peer(n), b)
        ).wait_recv()
        copy = remote(
            x_s.at[here, :, :, lanes], x_s.at[there, :, :, lanes], mate_s.at[n], mate_r.at[n], mate
        )
        copy.start()
        to_mate.append(copy)
    for load in loads[:2]:
        load.wait()
    for push in pushes[:3]:
        push.wait()

    other_rows = pl.ds(pl.multiple_of((1 - core) * FEAT, FEAT), FEAT)

    def up_first(lanes_of, add):
        tokens = x_s[pl.ds(0, 2), :, :, lanes_of].reshape(128, FEAT)
        for lo in range(0, UP, 512):
            hi = min(lo + 512, UP)
            part = jnp.dot(tokens, up_w[lanes_of, lo:hi], preferred_element_type=F32)
            part = part.reshape(2, 2, 32, hi - lo)
            pu[0:2, :, :, lo:hi] = pu[0:2, :, :, lo:hi] + part if add else part

    up_first(rows, False)
    for copy in to_mate:
        copy.wait_recv()
    pushes[3].start()
    up_first(other_rows, True)

    lane = lax.broadcasted_iota(jnp.int32, (32, 128), 1)

    def project(s):
        tokens = x_s[pl.ds(s * 2, 2)].reshape(128, 2 * FEAT)
        return tokens

    def up_pair(s):
        tokens = project(s)
        for lo in range(0, UP, 512):
            hi = min(lo + 512, UP)
            part = jnp.dot(tokens, up_w[:, lo:hi], preferred_element_type=F32)
            pu[pl.ds(s * 2, 2), :, :, lo:hi] = part.reshape(2, 2, 32, hi - lo)
        square_sums(s)

    def square_sums(s):
        tokens = project(s)
        plain = [
            tokens[:, c * FEAT : (c + 1) * FEAT].astype(F32) * inv_gain[c, 0:1] for c in range(2)
        ]
        squares = plain[0] * plain[0] + plain[1] * plain[1]
        total = jnp.sum(squares, axis=1, keepdims=True)
        pu[pl.ds(s * 2, 2), :, :, UP:] = jnp.broadcast_to(total, (128, 128)).reshape(2, 2, 32, 128)

    def gate_pair(s):
        tokens = project(s)
        for lo in range(0, HALF, 512):
            hi = min(lo + 512, HALF)
            part = jnp.dot(tokens, gate_w[:, lo:hi], preferred_element_type=F32)
            pg[pl.ds(s * 2, 2), :, :, lo:hi] = part.reshape(2, 2, 32, hi - lo)
        part = jnp.dot(tokens, up_w[:, UP:], preferred_element_type=F32)
        pg[pl.ds(s * 2, 2), :, :, HALF:] = part.reshape(2, 2, 32, TAIL)
        xg_send[pl.ds(s * 2, 2)] = pg[pl.ds(s * 2, 2), x_other].astype(BF16)

    def xg_copy(n):
        return remote(xg_send.at[n], xg_recv.at[n], xg_ss.at[n], xg_rs.at[n], xmate)

    def up_sum(block, half, arrived):
        body = pu[block, half, :, :UP]
        squares = pu[block, half, :, UP:]
        for ref in arrived:
            body = body + ref[:, :UP].astype(F32)
            halves = ref[:, UP:].astype(F32)
            squares = squares + halves + pltpu.roll(halves, 64, 1)
        return body, squares

    def put_up(ref, body, squares):
        ref[:, :UP] = body.astype(BF16)
        high = squares.astype(BF16)
        low = (squares - high.astype(F32)).astype(BF16)
        ref[:, UP:] = jnp.where(lane < 64, high.astype(F32), low.astype(F32)).astype(BF16)

    halves = (x_other, x)
    sent = []

    def ua_copy(s, n):
        h = halves[n]
        return remote(ua_send.at[s, h], ua_recv.at[s, h], ua_ss.at[s, n], ua_rs.at[s, n], ahead)

    def ub_copy(s, n):
        h = halves[n]
        return remote(ub_send.at[s, h], ub_recv.at[s, h], ub_ss.at[s, n], ub_rs.at[s, n], behind)

    def ga_copy(s):
        return remote(ga_send.at[s], ga_recv.at[s], ga_ss.at[s], ga_rs.at[s], ahead)

    def gb_copy(s):
        return remote(gb_send.at[s], gb_recv.at[s], gb_ss.at[s], gb_rs.at[s], behind)

    def up_step(s, n):
        h = halves[n]
        if s > 0:
            ua_copy(s - 1, n).wait_recv()
        arrived = [ua_recv.at[s - 1, h]] if s > 0 else []
        put_up(ua_send.at[s, h], *up_sum(2 * s, h, arrived))
        ua_copy(s, n).start()
        sent.append(ua_copy(s, n))
        if s < 3:
            if s > 0:
                ub_copy(s - 1, n).wait_recv()
            arrived = [ub_recv.at[s - 1, h]] if s > 0 else []
            put_up(ub_send.at[s, h], *up_sum(2 * s + 1, h, arrived))
            ub_copy(s, n).start()
            sent.append(ub_copy(s, n))

    def gate_step(s):
        xg_copy(2 * s).wait_recv()
        if s > 0:
            ga_copy(s - 1).wait_recv()
        total = pg[2 * s, x] + xg_recv[2 * s].astype(F32)
        if s > 0:
            total = total + ga_recv[s - 1].astype(F32)
        ga_send[s] = total.astype(BF16)
        ga_copy(s).start()
        sent.append(ga_copy(s))
        if s < 3:
            xg_copy(2 * s + 1).wait_recv()
            if s > 0:
                gb_copy(s - 1).wait_recv()
            total = pg[2 * s + 1, x] + xg_recv[2 * s + 1].astype(F32)
            if s > 0:
                total = total + gb_recv[s - 1].astype(F32)
            gb_send[s] = total.astype(BF16)
            gb_copy(s).start()
            sent.append(gb_copy(s))

    def gate_out(s):
        gate_pair(s)
        xg_copy(2 * s).start()
        xg_copy(2 * s + 1).start()

    square_sums(0)
    up_step(0, 0)
    up_step(0, 1)
    gate_out(0)
    gate_out(1)
    up_pair(1)
    up_step(1, 0)
    gate_out(2)
    gate_step(0)
    up_step(1, 1)
    up_pair(2)
    up_step(2, 0)
    gate_out(3)
    gate_step(1)
    up_pair(3)
    up_step(2, 1)
    up_step(3, 0)
    gate_step(2)
    up_step(3, 1)
    gate_step(3)

    xu_copy = remote(xu_send, xu_recv, xu_ss, xu_rs, xmate)
    for n in range(2):
        ua_copy(3, n).wait_recv()
        ub_copy(2, n).wait_recv()
        h = halves[n]
        body, squares = up_sum(7, h, [ua_recv.at[3, h], ub_recv.at[2, h]])
        if n == 0:
            put_up(xu_send, body, squares)
            xu_copy.start()
        else:
            pu[7, h, :, :UP] = body
            pu[7, h, :, UP:] = squares
    xg_copy(7).wait_recv()
    ga_copy(3).wait_recv()
    gb_copy(2).wait_recv()
    gate_sum = pg[7, x] + xg_recv[7].astype(F32) + ga_recv[3].astype(F32) + gb_recv[2].astype(F32)
    xu_copy.wait_recv()
    up_total, squares = up_sum(7, x, [xu_recv])
    scale = lax.rsqrt(squares[:, 0:1] / D + 1e-05)
    up_total = jnp.concatenate([up_total, gate_sum[:, HALF:]], axis=1)
    gate_sum = gate_sum[:, :HALF] * scale
    hidden = (gate_sum / (1.0 + jnp.exp(-gate_sum)) * (up_total * scale)).astype(BF16)
    h1[0, x] = hidden[:, :C1]
    h2[0, x] = hidden[:, C1:]

    def hidden_ref(kind, pos):
        return (h1.at[pos, x], h1.at[pos, x_other], h2.at[pos, x])[kind]

    def hz_copy(kind, pos, target, to):
        return remote(
            hidden_ref(kind, pos), hidden_ref(kind, target), hz_s.at[kind, target], hz_r.at[kind, target], to
        )

    def hx_copy(n, ref):
        return remote(ref, ref, hx_s.at[n], hx_r.at[n], xmate)

    def forward(kind, pos):
        if pos == 0:
            targets = ((1, ahead), (2, behind))
        elif pos % 2 == 1:
            targets = ((pos + 2, ahead),) if pos < 7 else ()
        else:
            targets = ((pos + 2, behind),) if pos < 6 else ()
        for target, to in targets:
            copy = hz_copy(kind, pos, target, to)
            copy.start()
            sent.append(copy)

    def to_xmate(pos):
        copy = hx_copy(pos, h2.at[pos, x])
        copy.start()
        sent.append(copy)

    def step_blocks(k):
        return (0, 1) if k == 0 else (2 * k - 1, 2 if k < 4 else 1)

    def mate_sums(k):
        some = pl.ds(0, step_blocks(k)[1] * 64)
        return remote(dp.at[k, 1 - core, some], dr.at[k, some], dr_s.at[k], dr_r.at[k], mate)

    def down_parts(k):
        first, count = step_blocks(k)

        def part(n):
            if n == 0:
                for pos in range(first, first + count):
                    hx_copy(pos, h2.at[pos, x_other]).wait_recv()
            c, cols = n // 2, slice(n % 2 * 256, n % 2 * 256 + 256)
            left = h1[first : first + count].reshape(count * 64, C1)
            right = h2[first : first + count].reshape(count * 64, C2)
            dp[k, c, : count * 64, cols] = jnp.dot(
                left, down_w[c, :C1, cols], preferred_element_type=F32
            ) + jnp.dot(right, down_w[c, C1:, cols], preferred_element_type=F32)
            if n == 3:
                mate_sums(k).start()
                sent.append(mate_sums(k))

        return [functools.partial(part, n) for n in range(4)]

    def return_copy(pos, owner):
        return remote(ds_send.at[pos], fr.at[g], fr_s.at[pos], fr_r.at[g], (owner, b))

    returns = []

    def return_parts(k):
        first, count = step_blocks(k)

        def part(j):
            if j == 0:
                mate_sums(k).wait_recv()
            pos = first + j
            there = count - 1 - j
            total = (
                dp[k, core, j * 64 : j * 64 + 64] + dr[k, there * 64 : there * 64 + 64]
            ).astype(BF16)
            ds_send[pos] = total
            owner = lax.rem(z + (-sign if j == 0 else sign) * k + RING, RING)
            returns.append((pos, owner))

            @pl.when(owner != g)
            def _():
                return_copy(pos, owner).start()

            @pl.when(owner == g)
            def _():
                fr[g] = total

        return [functools.partial(part, j) for j in range(count)]

    forward(2, 0)
    forward(0, 0)
    copy = hx_copy(8, h1.at[0, x])
    copy.start()
    sent.append(copy)
    to_xmate(0)
    pushes[3].wait()
    loads[2].wait()
    hx_copy(8, h1.at[0, x_other]).wait_recv()
    forward(1, 0)
    for k in range(1, 5):
        parts = down_parts(k - 1)
        if k >= 2:
            parts = return_parts(k - 2) + parts
        arrivals = [(kind, pos) for kind in (2, 0, 1) for pos in ((2 * k - 1, 2 * k) if k < 4 else (7,))]
        for n, (kind, pos) in enumerate(arrivals):
            hz_copy(kind, pos, pos, ahead).wait_recv()
            forward(kind, pos)
            if kind == 2:
                to_xmate(pos)
            due = (n + 1) * len(parts) // len(arrivals) - n * len(parts) // len(arrivals)
            for part in parts[n * len(parts) // len(arrivals) :][:due]:
                part()
    for part in down_parts(4) + return_parts(3) + return_parts(4):
        part()

    total = wide_s[...]
    for n in ORDER:
        remote(
            ds_send.at[0], fr.at[source(n)], fr_s.at[0], fr_r.at[source(n)], (peer(n), b)
        ).wait_recv()
    for j in range(GROUPS):
        total = total + fr[j].astype(F32)
    out[...] = total

    for copy in merges + gathers + to_mate:
        copy.wait_send()
    for n in range(8):
        xg_copy(n).wait_send()
    xu_copy.wait_send()
    for copy in sent:
        copy.wait_send()
    for pos, owner in returns:

        @pl.when(owner != g)
        def _():
            return_copy(pos, owner).wait_send()


def layer(queries, keys, values, key_new, value_new, lengths, res, gain, gate, up, down):
    vmem = pl.BlockSpec(memory_space=pltpu.VMEM)
    hbm = pl.BlockSpec(memory_space=pl.ANY)
    V = pltpu.VMEM
    dma = lambda *shape: pltpu.SemaphoreType.DMA(shape)
    scratch = [
        V((64, 2048), BF16), V((64, 64, 128), BF16), V((64, 64, 128), BF16),
        V((64, 128), BF16), V((64, 128), BF16), pltpu.SMEM((64,), jnp.int32),
        V((64, FEAT), BF16), V((FEAT,), BF16),
        V((64, 2048), F32), V((64, 128), F32), V((64, 128), F32), V((16, 64, 128), F32),
        V((128, 128), F32), V((4, 4, 64, 128), BF16), V((32, 128), F32),
        V((4, 4, 64, 128), BF16), V((128, 128), F32), V((64, FEAT), F32), V((2, 32, FEAT), BF16),
        V((2, 8, FEAT), F32),
        V((2 * FEAT, HALF), BF16), V((2 * FEAT, HALF), BF16), V((2, HALF, FEAT), BF16),
        V((8, 2, 32, 2 * FEAT), BF16), V((8, 2, 32, WIDE), F32), V((8, 2, 32, GATE), F32),
        V((8, 32, GATE), BF16), V((8, 32, GATE), BF16),
        V((4, 2, 32, WIDE), BF16), V((4, 2, 32, WIDE), BF16),
        V((3, 2, 32, WIDE), BF16), V((3, 2, 32, WIDE), BF16),
        V((4, 32, GATE), BF16), V((4, 32, GATE), BF16),
        V((3, 32, GATE), BF16), V((3, 32, GATE), BF16),
        V((32, WIDE), BF16), V((32, WIDE), BF16),
        V((8, 2, 32, C1), BF16), V((8, 2, 32, C2), BF16),
        V((5, 2, 128, FEAT), F32), V((5, 128, FEAT), F32),
        V((8, 64, FEAT), BF16), V((8, 64, FEAT), BF16),
        dma(8), dma(3), dma(4), dma(4), dma(8), dma(8), dma(8), dma(8), dma(8), dma(8),
        dma(8), dma(8), dma(4, 2), dma(4, 2), dma(3, 2), dma(3, 2),
        dma(4), dma(4), dma(3), dma(3), pltpu.SemaphoreType.DMA, pltpu.SemaphoreType.DMA,
        dma(3, 8), dma(3, 8), dma(9), dma(9), dma(5), dma(5), dma(8), dma(8),
    ]
    return pl.pallas_call(
        kernel,
        out_shape=pltpu.VMEM((64, FEAT), F32),
        in_specs=[hbm] * 11,
        out_specs=vmem,
        scratch_shapes=scratch,
        compiler_params=pltpu.CompilerParams(
            collective_id=0, has_side_effects=True, vmem_limit_bytes=61 * 1024 * 1024
        ),
        cost_estimate=pl.CostEstimate(
            flops=5_300_000_000, bytes_accessed=11_000_000, transcendentals=100_000
        ),
    )(queries, keys, values, key_new, value_new, lengths, res, gain, gate, up, down)


def on_device(
    residual_in,
    queries,
    key_cache,
    value_cache,
    key_new,
    value_new,
    lengths,
    ffn_gain,
    gate_weight,
    up_weight,
    down_weight,
):
    return layer(
        queries,
        key_cache,
        value_cache,
        key_new,
        value_new,
        lengths,
        residual_in,
        ffn_gain,
        gate_weight,
        up_weight,
        down_weight,
    )


def solution(mesh):
    in_specs = (
        P("grp", "blk"),
        P("grp", None),
        P("grp", "blk", None, None),
        P("grp", "blk", None, None),
        P("grp", None),
        P("grp", None),
        P("grp"),
        P("blk"),
        P("blk", "grp"),
        P("blk", "grp"),
        P("grp", "blk"),
    )
    out_specs = P("grp", "blk")
    return jax.shard_map(
        on_device, mesh=mesh, in_specs=in_specs, out_specs=out_specs, check_vma=False
    )
```

```python
import functools
import math

import jax
import jax.numpy as jnp
from jax import lax
from jax.experimental import pallas as pl
from jax.experimental.pallas import tpu as pltpu
from jax.sharding import PartitionSpec as P

D = 16384
HEADS = 128
KV_HEADS = 8
MESH = pl.DeviceIdType.MESH
F32 = jnp.float32
BF16 = jnp.bfloat16

RING = 8
GROUPS = 8
FEAT = 512
HALF = 1664
TAIL = 384
UP = HALF - TAIL
WIDE = UP + 128
GATE = HALF + TAIL
C1 = 768
C2 = HALF - C1


def slot_of(distance):
    return jnp.where(distance <= 4, 8 - 2 * distance, 2 * distance - 9)


def kernel(
    queries, keys, values, key_new, value_new, lengths, res_in, gain_in, gate, up, down, out,
    q_s, k_s, v_s, kn_s, vn_s, len_s, res, gain, q32, kn32, vn32, att, stats_s, w_in, st_in, w_got, st_got, wide_s, token_s, inv_gain,
    gate_w, up_w, down_w, x_s, pu, pg,
    xg_send, xg_recv, ua_send, ua_recv, ub_send, ub_recv,
    ga_send, ga_recv, gb_send, gb_recv, xu_send, xu_recv,
    h1, h2, dp, dr, ds_send, fr,
    load_sem, local_sem, wsem_s, wsem_r, at_s, at_r, tok_s, tok_r, mate_s, mate_r,
    xg_ss, xg_rs, ua_ss, ua_rs, ub_ss, ub_rs, ga_ss, ga_rs, gb_ss, gb_rs, xu_ss, xu_rs,
    hz_s, hz_r, hx_s, hx_r, dr_s, dr_r, fr_s, fr_r, fl_s, fl_r,
):
    g = lax.axis_index("grp")
    b = lax.axis_index("blk")
    z = b // 4
    q = b % 4
    x = q // 2
    core = q % 2
    sign = 1 - 2 * core
    mate = (g, z * 4 + x * 2 + (1 - core))
    xmate = (g, z * 4 + (1 - x) * 2 + core)
    ahead = (g, lax.rem(z + sign + RING, RING) * 4 + q)
    behind = (g, lax.rem(z - sign + RING, RING) * 4 + q)
    x_other = 1 - x

    def remote(src, dst, ss, rs, to):
        return pltpu.make_async_remote_copy(
            src_ref=src, dst_ref=dst, send_sem=ss, recv_sem=rs, device_id=to, device_id_type=MESH
        )

    def peer(n):
        return (lax.rem(g // 4 + n // 4, 2)) * 4 + lax.rem(g % 4 + n % 4, 4)

    def source(n):
        return (lax.rem(g // 4 + n // 4, 2)) * 4 + lax.rem(g % 4 - n % 4 + 4, 4)

    ORDER = (1, 3, 2, 4, 5, 7, 6)
    FAR_FIRST = (6, 5, 7, 4, 2, 1, 3)

    mine = pl.ds(pl.multiple_of(core * HALF, 128), HALF)
    other = pl.ds(pl.multiple_of((1 - core) * HALF, 128), HALF)
    rows = pl.ds(pl.multiple_of(core * FEAT, FEAT), FEAT)
    head_lanes = pl.ds(pl.multiple_of(z * 128, 128), 128)
    cache_loads = [
        pltpu.make_async_copy(
            queries.at[:, pl.ds(pl.multiple_of(z * 2048, 2048), 2048)], q_s, load_sem.at[0]
        ),
        pltpu.make_async_copy(key_new.at[:, head_lanes], kn_s, load_sem.at[1]),
        pltpu.make_async_copy(value_new.at[:, head_lanes], vn_s, load_sem.at[2]),
        pltpu.make_async_copy(lengths, len_s, load_sem.at[5]),
        pltpu.make_async_copy(keys.at[:, 0], k_s, load_sem.at[3]),
        pltpu.make_async_copy(values.at[:, 0], v_s, load_sem.at[4]),
        pltpu.make_async_copy(res_in, res, load_sem.at[6]),
        pltpu.make_async_copy(gain_in, gain, load_sem.at[7]),
    ]
    for load in cache_loads:
        load.start()
    loads = [
        pltpu.make_async_copy(gate.at[:, mine], gate_w.at[rows], local_sem.at[0]),
        pltpu.make_async_copy(up.at[:, mine], up_w.at[rows], local_sem.at[1]),
        pltpu.make_async_copy(down.at[mine], down_w.at[core], local_sem.at[2]),
    ]
    st_got[...] = jnp.zeros((128, 128), F32)
    barrier = pltpu.get_barrier_semaphore()
    partners = [mate, xmate, (g, z * 4 + (1 - x) * 2 + (1 - core)), ahead, behind]
    partners += [(peer(n), b) for n in ORDER]
    for partner in partners:
        pl.semaphore_signal(barrier, inc=1, device_id=partner, device_id_type=MESH)

    pl.semaphore_wait(barrier, len(partners))

    pushes = [
        remote(inv_gain.at[core], inv_gain.at[core], wsem_s.at[0], wsem_r.at[0], mate),
        remote(up.at[:, other], up_w.at[rows], wsem_s.at[1], wsem_r.at[1], mate),
        remote(gate.at[:, other], gate_w.at[rows], wsem_s.at[2], wsem_r.at[2], mate),
        remote(down.at[other], down_w.at[core], wsem_s.at[3], wsem_r.at[3], mate),
    ]
    for load in cache_loads:
        load.wait()
    for load in loads[:2]:
        load.start()
    gain_row = gain[...].astype(F32).reshape(1, FEAT)
    inv_gain[core] = jnp.broadcast_to(1.0 / gain_row, (8, FEAT))
    for push in pushes[:3]:
        push.start()
    loads[2].start()
    q32[...] = q_s[...].astype(F32)
    kn32[...] = kn_s[...].astype(F32)
    vn32[...] = vn_s[...].astype(F32)
    score_scale = 1.0 / math.sqrt(128)
    lane8 = lax.broadcasted_iota(jnp.int32, (8, 128), 1)
    row8 = lax.broadcasted_iota(jnp.int32, (8, 128), 0)
    row = lax.broadcasted_iota(jnp.int32, (128, 512), 0)
    col = lax.broadcasted_iota(jnp.int32, (128, 512), 1)
    same = lax.rem(row, 8) == col // 64
    place = q * 64 + lax.rem(col, 64)

    def attend(i, carry):
        eight = pl.ds(pl.multiple_of(i * 8, 8), 8)
        q8 = q32[eight]
        q_rows = jnp.concatenate([q8[:, h * 128 : h * 128 + 128] for h in range(16)], axis=0)
        k_rows = k_s[eight].reshape(512, 128)
        v_rows = v_s[eight].reshape(512, 128)
        spread = lambda a: jnp.concatenate([a] * 16, axis=0)
        limit = jnp.zeros((8, 128), jnp.int32)
        for n in range(8):
            limit = jnp.where(row8 == n, len_s[i * 8 + n], limit)
        usable = same & (place < spread(limit)[:, 0:1])
        scores = lax.dot_general(
            q_rows.astype(BF16), k_rows, (((1,), (1,)), ((), ())), preferred_element_type=F32
        )
        scores = jnp.where(usable, scores * score_scale, -1e30)
        fresh = jnp.sum(q_rows * spread(kn32[eight]), axis=1, keepdims=True) * score_scale
        fresh = jnp.where(q == 0, fresh, -1e30)
        top = jnp.maximum(jnp.max(scores, axis=1, keepdims=True), fresh)
        weights = jnp.where(usable, jnp.exp(scores - top), 0.0)
        fresh_weight = jnp.where(q == 0, jnp.exp(fresh - top), 0.0)
        total = jnp.sum(weights, axis=1, keepdims=True) + fresh_weight
        mixed = jnp.dot(weights.astype(BF16), v_rows, preferred_element_type=F32)
        mixed = mixed + fresh_weight * spread(vn32[eight])
        att[:, eight] = mixed.reshape(16, 8, 128)
        stats = jnp.zeros((8, 128), F32)
        for h in range(16):
            at = h // 4 * 8 + h % 4
            stats = jnp.where(lane8 == at, top[h * 8 : h * 8 + 8], stats)
            stats = jnp.where(lane8 == at + 4, total[h * 8 : h * 8 + 8], stats)
        stats_s[eight] = stats
        return carry

    stats_s[64:] = jnp.zeros((64, 128), F32)
    lax.fori_loop(0, 8, attend, 0, unroll=8)
    st_in[...] = jnp.transpose(stats_s[...])[:32]
    w_in[...] = att[...].astype(BF16).reshape(4, 4, 64, 128)

    eight_of = lambda n: pl.ds(pl.multiple_of(n * 8, 8), 8)
    merges = []
    for n in (3, 2, 1):
        p = q ^ n
        to = (g, z * 4 + p)
        merges.append(remote(st_in.at[eight_of(p)], st_got.at[eight_of(q)], at_s.at[n], at_r.at[q], to))
        merges.append(remote(w_in.at[p], w_got.at[q], at_s.at[4 + n], at_r.at[4 + q], to))
    for copy in merges:
        copy.start()
    st_got[eight_of(q)] = st_in[eight_of(q)]
    w_got[q] = w_in[q]
    for n in (1, 2, 3):
        p = q ^ n
        to = (g, z * 4 + p)
        remote(
            st_in.at[eight_of(p)], st_got.at[eight_of(p)], at_s.at[n], at_r.at[p], to
        ).wait_recv()
        remote(w_in.at[p], w_got.at[p], at_s.at[4 + n], at_r.at[4 + p], to).wait_recv()
    got = jnp.transpose(st_got[...])[:64]
    for head in range(4):
        cols = slice(head * 128, head * 128 + 128)
        tops = [got[:, j * 8 + head : j * 8 + head + 1] for j in range(4)]
        sums = [got[:, j * 8 + head + 4 : j * 8 + head + 5] for j in range(4)]
        top = jnp.maximum(jnp.maximum(tops[0], tops[1]), jnp.maximum(tops[2], tops[3]))
        factors = [jnp.exp(t - top) for t in tops]
        total = sum(f * s for f, s in zip(factors, sums))
        mixed = sum(f * w_got[j, head].astype(F32) for j, f in enumerate(factors))
        wide = res[:, cols].astype(F32) + mixed / total
        wide_s[:, cols] = wide
        scaled = (wide * gain_row[:, cols]).astype(BF16)
        token_s[0, :, cols] = scaled[:32]
        token_s[1, :, cols] = scaled[32:]

    def slots(owner):
        away = lax.rem((owner - z) * sign + 2 * RING - 1, RING) + 1
        back = lax.rem(RING - away + RING - 1, RING) + 1
        return slot_of(away), slot_of(back)

    lanes = pl.ds(pl.multiple_of(core * FEAT, FEAT), FEAT)
    own_slot, own_mate_slot = slots(g)
    gathers = []
    for n in FAR_FIRST:
        gathers.append(
            remote(token_s, x_s.at[own_slot, :, :, lanes], tok_s.at[n], tok_r.at[n], (peer(n), b))
        )
    for copy in gathers:
        copy.start()
    x_s[own_slot, :, :, lanes] = token_s[...]
    to_mate = [remote(token_s, x_s.at[own_mate_slot, :, :, lanes], mate_s.at[0], mate_r.at[0], mate)]
    to_mate[0].start()
    for n in FAR_FIRST:
        here, there = slots(source(n))
        remote(
            token_s, x_s.at[here, :, :, lanes], tok_s.at[n], tok_r.at[n], (peer(n), b)
        ).wait_recv()
        copy = remote(
            x_s.at[here, :, :, lanes], x_s.at[there, :, :, lanes], mate_s.at[n], mate_r.at[n], mate
        )
        copy.start()
        to_mate.append(copy)
    for load in loads[:2]:
        load.wait()
    for push in pushes[:3]:
        push.wait()

    other_rows = pl.ds(pl.multiple_of((1 - core) * FEAT, FEAT), FEAT)

    def up_first(lanes_of, add):
        tokens = x_s[pl.ds(0, 2), :, :, lanes_of].reshape(128, FEAT)
        for lo in range(0, UP, 512):
            hi = min(lo + 512, UP)
            part = jnp.dot(tokens, up_w[lanes_of, lo:hi], preferred_element_type=F32)
            part = part.reshape(2, 2, 32, hi - lo)
            pu[0:2, :, :, lo:hi] = pu[0:2, :, :, lo:hi] + part if add else part

    up_first(rows, False)
    for copy in to_mate:
        copy.wait_recv()
    pushes[3].start()
    up_first(other_rows, True)

    lane = lax.broadcasted_iota(jnp.int32, (32, 128), 1)

    def project(s):
        tokens = x_s[pl.ds(s * 2, 2)].reshape(128, 2 * FEAT)
        return tokens

    def up_pair(s):
        tokens = project(s)
        for lo in range(0, UP, 512):
            hi = min(lo + 512, UP)
            part = jnp.dot(tokens, up_w[:, lo:hi], preferred_element_type=F32)
            pu[pl.ds(s * 2, 2), :, :, lo:hi] = part.reshape(2, 2, 32, hi - lo)
        square_sums(s)

    def square_sums(s):
        tokens = project(s)
        plain = [
            tokens[:, c * FEAT : (c + 1) * FEAT].astype(F32) * inv_gain[c, 0:1] for c in range(2)
        ]
        squares = plain[0] * plain[0] + plain[1] * plain[1]
        total = jnp.sum(squares, axis=1, keepdims=True)
        pu[pl.ds(s * 2, 2), :, :, UP:] = jnp.broadcast_to(total, (128, 128)).reshape(2, 2, 32, 128)

    def gate_pair(s):
        tokens = project(s)
        for lo in range(0, HALF, 512):
            hi = min(lo + 512, HALF)
            part = jnp.dot(tokens, gate_w[:, lo:hi], preferred_element_type=F32)
            pg[pl.ds(s * 2, 2), :, :, lo:hi] = part.reshape(2, 2, 32, hi - lo)
        part = jnp.dot(tokens, up_w[:, UP:], preferred_element_type=F32)
        pg[pl.ds(s * 2, 2), :, :, HALF:] = part.reshape(2, 2, 32, TAIL)
        xg_send[pl.ds(s * 2, 2)] = pg[pl.ds(s * 2, 2), x_other].astype(BF16)

    def xg_copy(n):
        return remote(xg_send.at[n], xg_recv.at[n], xg_ss.at[n], xg_rs.at[n], xmate)

    def up_sum(block, half, arrived):
        body = pu[block, half, :, :UP]
        squares = pu[block, half, :, UP:]
        for ref in arrived:
            body = body + ref[:, :UP].astype(F32)
            halves = ref[:, UP:].astype(F32)
            squares = squares + halves + pltpu.roll(halves, 64, 1)
        return body, squares

    def put_up(ref, body, squares):
        ref[:, :UP] = body.astype(BF16)
        high = squares.astype(BF16)
        low = (squares - high.astype(F32)).astype(BF16)
        ref[:, UP:] = jnp.where(lane < 64, high.astype(F32), low.astype(F32)).astype(BF16)

    halves = (x_other, x)
    sent = []

    def ua_copy(s, n):
        h = halves[n]
        return remote(ua_send.at[s, h], ua_recv.at[s, h], ua_ss.at[s, n], ua_rs.at[s, n], ahead)

    def ub_copy(s, n):
        h = halves[n]
        return remote(ub_send.at[s, h], ub_recv.at[s, h], ub_ss.at[s, n], ub_rs.at[s, n], behind)

    def ga_copy(s):
        return remote(ga_send.at[s], ga_recv.at[s], ga_ss.at[s], ga_rs.at[s], ahead)

    def gb_copy(s):
        return remote(gb_send.at[s], gb_recv.at[s], gb_ss.at[s], gb_rs.at[s], behind)

    def up_step(s, n):
        h = halves[n]
        if s > 0:
            ua_copy(s - 1, n).wait_recv()
        arrived = [ua_recv.at[s - 1, h]] if s > 0 else []
        put_up(ua_send.at[s, h], *up_sum(2 * s, h, arrived))
        ua_copy(s, n).start()
        sent.append(ua_copy(s, n))
        if s < 3:
            if s > 0:
                ub_copy(s - 1, n).wait_recv()
            arrived = [ub_recv.at[s - 1, h]] if s > 0 else []
            put_up(ub_send.at[s, h], *up_sum(2 * s + 1, h, arrived))
            ub_copy(s, n).start()
            sent.append(ub_copy(s, n))

    def gate_step(s):
        xg_copy(2 * s).wait_recv()
        if s > 0:
            ga_copy(s - 1).wait_recv()
        total = pg[2 * s, x] + xg_recv[2 * s].astype(F32)
        if s > 0:
            total = total + ga_recv[s - 1].astype(F32)
        ga_send[s] = total.astype(BF16)
        ga_copy(s).start()
        sent.append(ga_copy(s))
        if s < 3:
            xg_copy(2 * s + 1).wait_recv()
            if s > 0:
                gb_copy(s - 1).wait_recv()
            total = pg[2 * s + 1, x] + xg_recv[2 * s + 1].astype(F32)
            if s > 0:
                total = total + gb_recv[s - 1].astype(F32)
            gb_send[s] = total.astype(BF16)
            gb_copy(s).start()
            sent.append(gb_copy(s))

    def gate_out(s):
        gate_pair(s)
        xg_copy(2 * s).start()
        xg_copy(2 * s + 1).start()

    square_sums(0)
    up_step(0, 0)
    up_step(0, 1)
    gate_out(0)
    gate_out(1)
    up_pair(1)
    up_step(1, 0)
    gate_out(2)
    gate_step(0)
    up_step(1, 1)
    up_pair(2)
    up_step(2, 0)
    gate_out(3)
    gate_step(1)
    up_pair(3)
    up_step(2, 1)
    up_step(3, 0)
    gate_step(2)
    up_step(3, 1)
    gate_step(3)

    xu_copy = remote(xu_send, xu_recv, xu_ss, xu_rs, xmate)
    for n in range(2):
        ua_copy(3, n).wait_recv()
        ub_copy(2, n).wait_recv()
        h = halves[n]
        body, squares = up_sum(7, h, [ua_recv.at[3, h], ub_recv.at[2, h]])
        if n == 0:
            put_up(xu_send, body, squares)
            xu_copy.start()
        else:
            pu[7, h, :, :UP] = body
            pu[7, h, :, UP:] = squares
    xg_copy(7).wait_recv()
    ga_copy(3).wait_recv()
    gb_copy(2).wait_recv()
    gate_sum = pg[7, x] + xg_recv[7].astype(F32) + ga_recv[3].astype(F32) + gb_recv[2].astype(F32)
    xu_copy.wait_recv()
    up_total, squares = up_sum(7, x, [xu_recv])
    scale = lax.rsqrt(squares[:, 0:1] / D + 1e-05)
    up_total = jnp.concatenate([up_total, gate_sum[:, HALF:]], axis=1)
    gate_sum = gate_sum[:, :HALF] * scale
    hidden = (gate_sum / (1.0 + jnp.exp(-gate_sum)) * (up_total * scale)).astype(BF16)
    h1[0, x] = hidden[:, :C1]
    h2[0, x] = hidden[:, C1:]

    def hidden_ref(kind, pos):
        return (h1.at[pos, x], h1.at[pos, x_other], h2.at[pos, x])[kind]

    def hz_copy(kind, pos, target, to):
        return remote(
            hidden_ref(kind, pos), hidden_ref(kind, target), hz_s.at[kind, target], hz_r.at[kind, target], to
        )

    def hx_copy(n, ref):
        return remote(ref, ref, hx_s.at[n], hx_r.at[n], xmate)

    def forward(kind, pos):
        if pos == 0:
            targets = ((1, ahead), (2, behind))
        elif pos % 2 == 1:
            targets = ((pos + 2, ahead),) if pos < 7 else ()
        else:
            targets = ((pos + 2, behind),) if pos < 6 else ()
        for target, to in targets:
            copy = hz_copy(kind, pos, target, to)
            copy.start()
            sent.append(copy)

    def to_xmate(pos):
        copy = hx_copy(pos, h2.at[pos, x])
        copy.start()
        sent.append(copy)

    def step_blocks(k):
        return (0, 1) if k == 0 else (2 * k - 1, 2 if k < 4 else 1)

    def mate_sums(k):
        some = pl.ds(0, step_blocks(k)[1] * 64)
        return remote(dp.at[k, 1 - core, some], dr.at[k, some], dr_s.at[k], dr_r.at[k], mate)

    def down_parts(k):
        first, count = step_blocks(k)

        def part(n):
            if n == 0:
                for pos in range(first, first + count):
                    hx_copy(pos, h2.at[pos, x_other]).wait_recv()
            c, cols = n // 2, slice(n % 2 * 256, n % 2 * 256 + 256)
            left = h1[first : first + count].reshape(count * 64, C1)
            right = h2[first : first + count].reshape(count * 64, C2)
            dp[k, c, : count * 64, cols] = jnp.dot(
                left, down_w[c, :C1, cols], preferred_element_type=F32
            ) + jnp.dot(right, down_w[c, C1:, cols], preferred_element_type=F32)
            if n == 3:
                mate_sums(k).start()
                sent.append(mate_sums(k))

        return [functools.partial(part, n) for n in range(4)]

    def return_copy(pos, owner):
        return remote(ds_send.at[pos], fr.at[g], fr_s.at[pos], fr_r.at[g], (owner, b))

    returns = []

    def return_parts(k):
        first, count = step_blocks(k)

        def part(j):
            if j == 0:
                mate_sums(k).wait_recv()
            pos = first + j
            there = count - 1 - j
            total = (
                dp[k, core, j * 64 : j * 64 + 64] + dr[k, there * 64 : there * 64 + 64]
            ).astype(BF16)
            ds_send[pos] = total
            owner = lax.rem(z + (-sign if j == 0 else sign) * k + RING, RING)
            returns.append((pos, owner))

            @pl.when(owner != g)
            def _():
                return_copy(pos, owner).start()

            @pl.when(owner == g)
            def _():
                fr[g] = total

        return [functools.partial(part, j) for j in range(count)]

    own_rows = [pl.ds(pl.multiple_of(h * 32, 32), 32) for h in (x, x_other)]

    def owner_of(k, j):
        return lax.rem(z + (-sign if j == 0 else sign) * k + RING, RING)

    def half_sums(k, n):
        size = step_blocks(k)[1] * 32
        some = pl.ds(n * size, size)
        sem = 2 * k - 3 + n
        return remote(dp.at[k, 1 - core, some], dr.at[k, some], dr_s.at[sem], dr_r.at[sem], mate)

    def half_copy(k, j, n, slot):
        pos = 2 * k - 1 + j
        return remote(
            ds_send.at[pos, own_rows[n]],
            fr.at[slot, own_rows[n]],
            fl_s.at[pos - 5, n],
            fl_r.at[n, slot],
            (owner_of(k, j), b),
        )

    def half_down(k, n):
        first, count = step_blocks(k)
        h = (x, x_other)[n]
        if n == 1:
            for pos in range(first, first + count):
                hx_copy(pos, h2.at[pos, x_other]).wait_recv()
        left = h1[first : first + count, h].reshape(count * 32, C1)
        right = h2[first : first + count, h].reshape(count * 32, C2)
        for c in range(2):
            dp[k, c, n * count * 32 : (n + 1) * count * 32] = jnp.dot(
                left, down_w[c, :C1], preferred_element_type=F32
            ) + jnp.dot(right, down_w[c, C1:], preferred_element_type=F32)
        half_sums(k, n).start()
        sent.append(half_sums(k, n))

    def half_return(k, n):
        half_sums(k, n).wait_recv()
        first, count = step_blocks(k)
        for j in range(count):
            here = (n * count + j) * 32
            there = (n * count + count - 1 - j) * 32
            total = (dp[k, core, here : here + 32] + dr[k, there : there + 32]).astype(BF16)
            ds_send[first + j, own_rows[n]] = total
            owner = owner_of(k, j)

            @pl.when(owner != g)
            def _():
                half_copy(k, j, n, g).start()

            @pl.when(owner == g)
            def _():
                fr[g, own_rows[n]] = total

    forward(2, 0)
    forward(0, 0)
    copy = hx_copy(8, h1.at[0, x])
    copy.start()
    sent.append(copy)
    to_xmate(0)
    pushes[3].wait()
    loads[2].wait()
    hx_copy(8, h1.at[0, x_other]).wait_recv()
    forward(1, 0)
    for k in range(1, 4):
        parts = down_parts(k - 1)
        if k >= 2:
            parts = return_parts(k - 2) + parts
        arrivals = [(kind, pos) for kind in (2, 0, 1) for pos in (2 * k - 1, 2 * k)]
        for n, (kind, pos) in enumerate(arrivals):
            hz_copy(kind, pos, pos, ahead).wait_recv()
            forward(kind, pos)
            if kind == 2:
                to_xmate(pos)
            lo, hi = n * len(parts) // len(arrivals), (n + 1) * len(parts) // len(arrivals)
            for part in parts[lo:hi]:
                part()
    half_down(3, 0)
    hz_copy(2, 7, 7, ahead).wait_recv()
    to_xmate(7)
    for part in return_parts(2):
        part()
    half_return(3, 0)
    hz_copy(0, 7, 7, ahead).wait_recv()
    half_down(4, 0)
    half_down(3, 1)
    half_return(4, 0)
    hz_copy(1, 7, 7, ahead).wait_recv()
    half_return(3, 1)
    half_down(4, 1)
    half_return(4, 1)

    total = wide_s[...]
    away = lax.rem(z - g + RING, RING)
    in_halves = (away >= 3) & (away <= 5)

    @pl.when(in_halves)
    def _():
        for half in range(2):
            for n in ORDER:
                half_copy(4, 0, half, source(n)).wait_recv()

    @pl.when(jnp.logical_not(in_halves))
    def _():
        for n in ORDER:
            remote(
                ds_send.at[0], fr.at[source(n)], fr_s.at[0], fr_r.at[source(n)], (peer(n), b)
            ).wait_recv()

    for j in range(GROUPS):
        total = total + fr[j].astype(F32)
    out[...] = total

    for copy in merges + gathers + to_mate:
        copy.wait_send()
    for n in range(8):
        xg_copy(n).wait_send()
    xu_copy.wait_send()
    for copy in sent:
        copy.wait_send()
    for k, j in ((3, 0), (3, 1), (4, 0)):

        @pl.when(owner_of(k, j) != g)
        def _():
            half_copy(k, j, 0, g).wait_send()
            half_copy(k, j, 1, g).wait_send()

    for pos, owner in returns:

        @pl.when(owner != g)
        def _():
            return_copy(pos, owner).wait_send()


def layer(queries, keys, values, key_new, value_new, lengths, res, gain, gate, up, down):
    vmem = pl.BlockSpec(memory_space=pltpu.VMEM)
    hbm = pl.BlockSpec(memory_space=pl.ANY)
    V = pltpu.VMEM
    dma = lambda *shape: pltpu.SemaphoreType.DMA(shape)
    scratch = [
        V((64, 2048), BF16), V((64, 64, 128), BF16), V((64, 64, 128), BF16),
        V((64, 128), BF16), V((64, 128), BF16), pltpu.SMEM((64,), jnp.int32),
        V((64, FEAT), BF16), V((FEAT,), BF16),
        V((64, 2048), F32), V((64, 128), F32), V((64, 128), F32), V((16, 64, 128), F32),
        V((128, 128), F32), V((4, 4, 64, 128), BF16), V((32, 128), F32),
        V((4, 4, 64, 128), BF16), V((128, 128), F32), V((64, FEAT), F32), V((2, 32, FEAT), BF16),
        V((2, 8, FEAT), F32),
        V((2 * FEAT, HALF), BF16), V((2 * FEAT, HALF), BF16), V((2, HALF, FEAT), BF16),
        V((8, 2, 32, 2 * FEAT), BF16), V((8, 2, 32, WIDE), F32), V((8, 2, 32, GATE), F32),
        V((8, 32, GATE), BF16), V((8, 32, GATE), BF16),
        V((4, 2, 32, WIDE), BF16), V((4, 2, 32, WIDE), BF16),
        V((3, 2, 32, WIDE), BF16), V((3, 2, 32, WIDE), BF16),
        V((4, 32, GATE), BF16), V((4, 32, GATE), BF16),
        V((3, 32, GATE), BF16), V((3, 32, GATE), BF16),
        V((32, WIDE), BF16), V((32, WIDE), BF16),
        V((8, 2, 32, C1), BF16), V((8, 2, 32, C2), BF16),
        V((5, 2, 128, FEAT), F32), V((5, 128, FEAT), F32),
        V((8, 64, FEAT), BF16), V((8, 64, FEAT), BF16),
        dma(8), dma(3), dma(4), dma(4), dma(8), dma(8), dma(8), dma(8), dma(8), dma(8),
        dma(8), dma(8), dma(4, 2), dma(4, 2), dma(3, 2), dma(3, 2),
        dma(4), dma(4), dma(3), dma(3), pltpu.SemaphoreType.DMA, pltpu.SemaphoreType.DMA,
        dma(3, 8), dma(3, 8), dma(9), dma(9), dma(7), dma(7), dma(8), dma(8), dma(3, 2), dma(2, 8),
    ]
    return pl.pallas_call(
        kernel,
        out_shape=pltpu.VMEM((64, FEAT), F32),
        in_specs=[hbm] * 11,
        out_specs=vmem,
        scratch_shapes=scratch,
        compiler_params=pltpu.CompilerParams(
            collective_id=0, has_side_effects=True, vmem_limit_bytes=61 * 1024 * 1024
        ),
        cost_estimate=pl.CostEstimate(
            flops=5_300_000_000, bytes_accessed=11_000_000, transcendentals=100_000
        ),
    )(queries, keys, values, key_new, value_new, lengths, res, gain, gate, up, down)


def on_device(
    residual_in,
    queries,
    key_cache,
    value_cache,
    key_new,
    value_new,
    lengths,
    ffn_gain,
    gate_weight,
    up_weight,
    down_weight,
):
    return layer(
        queries,
        key_cache,
        value_cache,
        key_new,
        value_new,
        lengths,
        residual_in,
        ffn_gain,
        gate_weight,
        up_weight,
        down_weight,
    )


def solution(mesh):
    in_specs = (
        P("grp", "blk"),
        P("grp", None),
        P("grp", "blk", None, None),
        P("grp", "blk", None, None),
        P("grp", None),
        P("grp", None),
        P("grp"),
        P("blk"),
        P("blk", "grp"),
        P("blk", "grp"),
        P("grp", "blk"),
    )
    out_specs = P("grp", "blk")
    return jax.shard_map(
        on_device, mesh=mesh, in_specs=in_specs, out_specs=out_specs, check_vma=False
    )
```

```python
import functools
import math

import jax
import jax.numpy as jnp
from jax import lax
from jax.experimental import pallas as pl
from jax.experimental.pallas import tpu as pltpu
from jax.sharding import PartitionSpec as P

D = 16384
HEADS = 128
KV_HEADS = 8
MESH = pl.DeviceIdType.MESH
F32 = jnp.float32
BF16 = jnp.bfloat16

RING = 8
GROUPS = 8
FEAT = 512
HALF = 1664
TAIL = 512
UP = HALF - TAIL
WIDE = UP + 128
GATE = HALF + TAIL
C1 = 768
C2 = HALF - C1


def slot_of(distance):
    return jnp.where(distance <= 4, 8 - 2 * distance, 2 * distance - 9)


def kernel(
    queries, keys, values, key_new, value_new, lengths, res_in, gain_in, gate, up, down, out,
    q_s, k_s, v_s, kn_s, vn_s, len_s, res, gain, q32, kn32, vn32, att, stats_s, w_in, st_in, w_got, st_got, wide_s, token_s, inv_gain,
    gate_w, up_w, down_w, x_s, pu, pg,
    xg_send, xg_recv, ua_send, ua_recv, ub_send, ub_recv,
    ga_send, ga_recv, gb_send, gb_recv, xu_send, xu_recv,
    h1, h2, dp, dr, ds_send, fr,
    load_sem, local_sem, wsem_s, wsem_r, at_s, at_r, tok_s, tok_r, mate_s, mate_r,
    xg_ss, xg_rs, ua_ss, ua_rs, ub_ss, ub_rs, ga_ss, ga_rs, gb_ss, gb_rs, xu_ss, xu_rs,
    hz_s, hz_r, hx_s, hx_r, dr_s, dr_r, fr_s, fr_r, fl_s, fl_r,
):
    g = lax.axis_index("grp")
    b = lax.axis_index("blk")
    z = b // 4
    q = b % 4
    x = q // 2
    core = q % 2
    sign = 1 - 2 * core
    mate = (g, z * 4 + x * 2 + (1 - core))
    xmate = (g, z * 4 + (1 - x) * 2 + core)
    ahead = (g, lax.rem(z + sign + RING, RING) * 4 + q)
    behind = (g, lax.rem(z - sign + RING, RING) * 4 + q)
    x_other = 1 - x

    def remote(src, dst, ss, rs, to):
        return pltpu.make_async_remote_copy(
            src_ref=src, dst_ref=dst, send_sem=ss, recv_sem=rs, device_id=to, device_id_type=MESH
        )

    def peer(n):
        return (lax.rem(g // 4 + n // 4, 2)) * 4 + lax.rem(g % 4 + n % 4, 4)

    def source(n):
        return (lax.rem(g // 4 + n // 4, 2)) * 4 + lax.rem(g % 4 - n % 4 + 4, 4)

    ORDER = (1, 3, 2, 4, 5, 7, 6)
    FAR_FIRST = (6, 5, 7, 4, 2, 1, 3)

    mine = pl.ds(pl.multiple_of(core * HALF, 128), HALF)
    other = pl.ds(pl.multiple_of((1 - core) * HALF, 128), HALF)
    rows = pl.ds(pl.multiple_of(core * FEAT, FEAT), FEAT)
    head_lanes = pl.ds(pl.multiple_of(z * 128, 128), 128)
    cache_loads = [
        pltpu.make_async_copy(
            queries.at[:, pl.ds(pl.multiple_of(z * 2048, 2048), 2048)], q_s, load_sem.at[0]
        ),
        pltpu.make_async_copy(key_new.at[:, head_lanes], kn_s, load_sem.at[1]),
        pltpu.make_async_copy(value_new.at[:, head_lanes], vn_s, load_sem.at[2]),
        pltpu.make_async_copy(lengths, len_s, load_sem.at[5]),
        pltpu.make_async_copy(keys.at[:, 0], k_s, load_sem.at[3]),
        pltpu.make_async_copy(values.at[:, 0], v_s, load_sem.at[4]),
        pltpu.make_async_copy(res_in, res, load_sem.at[6]),
        pltpu.make_async_copy(gain_in, gain, load_sem.at[7]),
    ]
    for load in cache_loads:
        load.start()
    loads = [
        pltpu.make_async_copy(gate.at[:, mine], gate_w.at[rows], local_sem.at[0]),
        pltpu.make_async_copy(up.at[:, mine], up_w.at[rows], local_sem.at[1]),
        pltpu.make_async_copy(down.at[mine], down_w.at[core], local_sem.at[2]),
    ]
    st_got[...] = jnp.zeros((128, 128), F32)
    barrier = pltpu.get_barrier_semaphore()
    partners = [mate, xmate, (g, z * 4 + (1 - x) * 2 + (1 - core)), ahead, behind]
    partners += [(peer(n), b) for n in ORDER]
    for partner in partners:
        pl.semaphore_signal(barrier, inc=1, device_id=partner, device_id_type=MESH)

    pl.semaphore_wait(barrier, len(partners))

    pushes = [
        remote(inv_gain.at[core], inv_gain.at[core], wsem_s.at[0], wsem_r.at[0], mate),
        remote(up.at[:, other], up_w.at[rows], wsem_s.at[1], wsem_r.at[1], mate),
        remote(gate.at[:, other], gate_w.at[rows], wsem_s.at[2], wsem_r.at[2], mate),
        remote(down.at[other], down_w.at[core], wsem_s.at[3], wsem_r.at[3], mate),
    ]
    for load in cache_loads:
        load.wait()
    for load in loads[:2]:
        load.start()
    gain_row = gain[...].astype(F32).reshape(1, FEAT)
    inv_gain[core] = jnp.broadcast_to(1.0 / gain_row, (8, FEAT))
    for push in pushes[:3]:
        push.start()
    loads[2].start()
    q32[...] = q_s[...].astype(F32)
    kn32[...] = kn_s[...].astype(F32)
    vn32[...] = vn_s[...].astype(F32)
    score_scale = 1.0 / math.sqrt(128)
    lane8 = lax.broadcasted_iota(jnp.int32, (8, 128), 1)
    row8 = lax.broadcasted_iota(jnp.int32, (8, 128), 0)
    row = lax.broadcasted_iota(jnp.int32, (128, 512), 0)
    col = lax.broadcasted_iota(jnp.int32, (128, 512), 1)
    same = lax.rem(row, 8) == col // 64
    place = q * 64 + lax.rem(col, 64)

    def attend(i, carry):
        eight = pl.ds(pl.multiple_of(i * 8, 8), 8)
        q8 = q32[eight]
        q_rows = jnp.concatenate([q8[:, h * 128 : h * 128 + 128] for h in range(16)], axis=0)
        k_rows = k_s[eight].reshape(512, 128)
        v_rows = v_s[eight].reshape(512, 128)
        spread = lambda a: jnp.concatenate([a] * 16, axis=0)
        limit = jnp.zeros((8, 128), jnp.int32)
        for n in range(8):
            limit = jnp.where(row8 == n, len_s[i * 8 + n], limit)
        usable = same & (place < spread(limit)[:, 0:1])
        scores = lax.dot_general(
            q_rows.astype(BF16), k_rows, (((1,), (1,)), ((), ())), preferred_element_type=F32
        )
        scores = jnp.where(usable, scores * score_scale, -1e30)
        fresh = jnp.sum(q_rows * spread(kn32[eight]), axis=1, keepdims=True) * score_scale
        fresh = jnp.where(q == 0, fresh, -1e30)
        top = jnp.maximum(jnp.max(scores, axis=1, keepdims=True), fresh)
        weights = jnp.where(usable, jnp.exp(scores - top), 0.0)
        fresh_weight = jnp.where(q == 0, jnp.exp(fresh - top), 0.0)
        total = jnp.sum(weights, axis=1, keepdims=True) + fresh_weight
        mixed = jnp.dot(weights.astype(BF16), v_rows, preferred_element_type=F32)
        mixed = mixed + fresh_weight * spread(vn32[eight])
        att[:, eight] = mixed.reshape(16, 8, 128)
        stats = jnp.zeros((8, 128), F32)
        for h in range(16):
            at = h // 4 * 8 + h % 4
            stats = jnp.where(lane8 == at, top[h * 8 : h * 8 + 8], stats)
            stats = jnp.where(lane8 == at + 4, total[h * 8 : h * 8 + 8], stats)
        stats_s[eight] = stats
        return carry

    stats_s[64:] = jnp.zeros((64, 128), F32)
    lax.fori_loop(0, 8, attend, 0, unroll=8)
    st_in[...] = jnp.transpose(stats_s[...])[:32]
    w_in[...] = att[...].astype(BF16).reshape(4, 4, 64, 128)

    eight_of = lambda n: pl.ds(pl.multiple_of(n * 8, 8), 8)
    merges = []
    for n in (3, 2, 1):
        p = q ^ n
        to = (g, z * 4 + p)
        merges.append(remote(st_in.at[eight_of(p)], st_got.at[eight_of(q)], at_s.at[n], at_r.at[q], to))
        merges.append(remote(w_in.at[p], w_got.at[q], at_s.at[4 + n], at_r.at[4 + q], to))
    for copy in merges:
        copy.start()
    st_got[eight_of(q)] = st_in[eight_of(q)]
    w_got[q] = w_in[q]
    for n in (1, 2, 3):
        p = q ^ n
        to = (g, z * 4 + p)
        remote(
            st_in.at[eight_of(p)], st_got.at[eight_of(p)], at_s.at[n], at_r.at[p], to
        ).wait_recv()
        remote(w_in.at[p], w_got.at[p], at_s.at[4 + n], at_r.at[4 + p], to).wait_recv()
    got = jnp.transpose(st_got[...])[:64]
    for head in range(4):
        cols = slice(head * 128, head * 128 + 128)
        tops = [got[:, j * 8 + head : j * 8 + head + 1] for j in range(4)]
        sums = [got[:, j * 8 + head + 4 : j * 8 + head + 5] for j in range(4)]
        top = jnp.maximum(jnp.maximum(tops[0], tops[1]), jnp.maximum(tops[2], tops[3]))
        factors = [jnp.exp(t - top) for t in tops]
        total = sum(f * s for f, s in zip(factors, sums))
        mixed = sum(f * w_got[j, head].astype(F32) for j, f in enumerate(factors))
        wide = res[:, cols].astype(F32) + mixed / total
        wide_s[:, cols] = wide
        scaled = (wide * gain_row[:, cols]).astype(BF16)
        token_s[0, :, cols] = scaled[:32]
        token_s[1, :, cols] = scaled[32:]

    def slots(owner):
        away = lax.rem((owner - z) * sign + 2 * RING - 1, RING) + 1
        back = lax.rem(RING - away + RING - 1, RING) + 1
        return slot_of(away), slot_of(back)

    lanes = pl.ds(pl.multiple_of(core * FEAT, FEAT), FEAT)
    own_slot, own_mate_slot = slots(g)
    gathers = []
    for n in FAR_FIRST:
        gathers.append(
            remote(token_s, x_s.at[own_slot, :, :, lanes], tok_s.at[n], tok_r.at[n], (peer(n), b))
        )
    for copy in gathers:
        copy.start()
    x_s[own_slot, :, :, lanes] = token_s[...]
    to_mate = [remote(token_s, x_s.at[own_mate_slot, :, :, lanes], mate_s.at[0], mate_r.at[0], mate)]
    to_mate[0].start()
    for n in FAR_FIRST:
        here, there = slots(source(n))
        remote(
            token_s, x_s.at[here, :, :, lanes], tok_s.at[n], tok_r.at[n], (peer(n), b)
        ).wait_recv()
        copy = remote(
            x_s.at[here, :, :, lanes], x_s.at[there, :, :, lanes], mate_s.at[n], mate_r.at[n], mate
        )
        copy.start()
        to_mate.append(copy)
    for load in loads[:2]:
        load.wait()
    for push in pushes[:3]:
        push.wait()

    other_rows = pl.ds(pl.multiple_of((1 - core) * FEAT, FEAT), FEAT)

    def up_first(lanes_of, add):
        tokens = x_s[pl.ds(0, 2), :, :, lanes_of].reshape(128, FEAT)
        for lo in range(0, UP, 512):
            hi = min(lo + 512, UP)
            part = jnp.dot(tokens, up_w[lanes_of, lo:hi], preferred_element_type=F32)
            part = part.reshape(2, 2, 32, hi - lo)
            pu[0:2, :, :, lo:hi] = pu[0:2, :, :, lo:hi] + part if add else part

    up_first(rows, False)
    for copy in to_mate:
        copy.wait_recv()
    pushes[3].start()
    up_first(other_rows, True)

    lane = lax.broadcasted_iota(jnp.int32, (32, 128), 1)

    def project(s):
        tokens = x_s[pl.ds(s * 2, 2)].reshape(128, 2 * FEAT)
        return tokens

    def up_pair(s):
        tokens = project(s)
        for lo in range(0, UP, 512):
            hi = min(lo + 512, UP)
            part = jnp.dot(tokens, up_w[:, lo:hi], preferred_element_type=F32)
            pu[pl.ds(s * 2, 2), :, :, lo:hi] = part.reshape(2, 2, 32, hi - lo)
        square_sums(s)

    def square_sums(s):
        tokens = project(s)
        plain = [
            tokens[:, c * FEAT : (c + 1) * FEAT].astype(F32) * inv_gain[c, 0:1] for c in range(2)
        ]
        squares = plain[0] * plain[0] + plain[1] * plain[1]
        total = jnp.sum(squares, axis=1, keepdims=True)
        pu[pl.ds(s * 2, 2), :, :, UP:] = jnp.broadcast_to(total, (128, 128)).reshape(2, 2, 32, 128)

    def gate_pair(s):
        tokens = project(s)
        for lo in range(0, HALF, 512):
            hi = min(lo + 512, HALF)
            part = jnp.dot(tokens, gate_w[:, lo:hi], preferred_element_type=F32)
            pg[pl.ds(s * 2, 2), :, :, lo:hi] = part.reshape(2, 2, 32, hi - lo)
        part = jnp.dot(tokens, up_w[:, UP:], preferred_element_type=F32)
        pg[pl.ds(s * 2, 2), :, :, HALF:] = part.reshape(2, 2, 32, TAIL)
        xg_send[pl.ds(s * 2, 2)] = pg[pl.ds(s * 2, 2), x_other].astype(BF16)

    def xg_copy(n):
        return remote(xg_send.at[n], xg_recv.at[n], xg_ss.at[n], xg_rs.at[n], xmate)

    def up_sum(block, half, arrived):
        body = pu[block, half, :, :UP]
        squares = pu[block, half, :, UP:]
        for ref in arrived:
            body = body + ref[:, :UP].astype(F32)
            halves = ref[:, UP:].astype(F32)
            squares = squares + halves + pltpu.roll(halves, 64, 1)
        return body, squares

    def put_up(ref, body, squares):
        ref[:, :UP] = body.astype(BF16)
        high = squares.astype(BF16)
        low = (squares - high.astype(F32)).astype(BF16)
        ref[:, UP:] = jnp.where(lane < 64, high.astype(F32), low.astype(F32)).astype(BF16)

    halves = (x_other, x)
    sent = []

    def ua_copy(s, n):
        h = halves[n]
        return remote(ua_send.at[s, h], ua_recv.at[s, h], ua_ss.at[s, n], ua_rs.at[s, n], ahead)

    def ub_copy(s, n):
        h = halves[n]
        return remote(ub_send.at[s, h], ub_recv.at[s, h], ub_ss.at[s, n], ub_rs.at[s, n], behind)

    def ga_copy(s):
        return remote(ga_send.at[s], ga_recv.at[s], ga_ss.at[s], ga_rs.at[s], ahead)

    def gb_copy(s):
        return remote(gb_send.at[s], gb_recv.at[s], gb_ss.at[s], gb_rs.at[s], behind)

    def up_step(s, n):
        h = halves[n]
        if s > 0:
            ua_copy(s - 1, n).wait_recv()
        arrived = [ua_recv.at[s - 1, h]] if s > 0 else []
        put_up(ua_send.at[s, h], *up_sum(2 * s, h, arrived))
        ua_copy(s, n).start()
        sent.append(ua_copy(s, n))
        if s < 3:
            if s > 0:
                ub_copy(s - 1, n).wait_recv()
            arrived = [ub_recv.at[s - 1, h]] if s > 0 else []
            put_up(ub_send.at[s, h], *up_sum(2 * s + 1, h, arrived))
            ub_copy(s, n).start()
            sent.append(ub_copy(s, n))

    def gate_step(s):
        xg_copy(2 * s).wait_recv()
        if s > 0:
            ga_copy(s - 1).wait_recv()
        total = pg[2 * s, x] + xg_recv[2 * s].astype(F32)
        if s > 0:
            total = total + ga_recv[s - 1].astype(F32)
        ga_send[s] = total.astype(BF16)
        ga_copy(s).start()
        sent.append(ga_copy(s))
        if s < 3:
            xg_copy(2 * s + 1).wait_recv()
            if s > 0:
                gb_copy(s - 1).wait_recv()
            total = pg[2 * s + 1, x] + xg_recv[2 * s + 1].astype(F32)
            if s > 0:
                total = total + gb_recv[s - 1].astype(F32)
            gb_send[s] = total.astype(BF16)
            gb_copy(s).start()
            sent.append(gb_copy(s))

    def gate_out(s):
        gate_pair(s)
        xg_copy(2 * s).start()
        xg_copy(2 * s + 1).start()

    square_sums(0)
    up_step(0, 0)
    up_step(0, 1)
    gate_out(0)
    gate_out(1)
    up_pair(1)
    up_step(1, 0)
    gate_out(2)
    gate_step(0)
    up_step(1, 1)
    up_pair(2)
    up_step(2, 0)
    gate_out(3)
    gate_step(1)
    up_pair(3)
    up_step(2, 1)
    up_step(3, 0)
    gate_step(2)
    up_step(3, 1)
    gate_step(3)

    xu_copy = remote(xu_send, xu_recv, xu_ss, xu_rs, xmate)
    for n in range(2):
        ua_copy(3, n).wait_recv()
        ub_copy(2, n).wait_recv()
        h = halves[n]
        body, squares = up_sum(7, h, [ua_recv.at[3, h], ub_recv.at[2, h]])
        if n == 0:
            put_up(xu_send, body, squares)
            xu_copy.start()
        else:
            pu[7, h, :, :UP] = body
            pu[7, h, :, UP:] = squares
    xg_copy(7).wait_recv()
    ga_copy(3).wait_recv()
    gb_copy(2).wait_recv()
    gate_sum = pg[7, x] + xg_recv[7].astype(F32) + ga_recv[3].astype(F32) + gb_recv[2].astype(F32)
    xu_copy.wait_recv()
    up_total, squares = up_sum(7, x, [xu_recv])
    scale = lax.rsqrt(squares[:, 0:1] / D + 1e-05)
    up_total = jnp.concatenate([up_total, gate_sum[:, HALF:]], axis=1)
    gate_sum = gate_sum[:, :HALF] * scale
    hidden = (gate_sum / (1.0 + jnp.exp(-gate_sum)) * (up_total * scale)).astype(BF16)
    h1[0, x] = hidden[:, :C1]
    h2[0, x] = hidden[:, C1:]

    def hidden_ref(kind, pos):
        return (h1.at[pos, x], h1.at[pos, x_other], h2.at[pos, x])[kind]

    def hz_copy(kind, pos, target, to):
        return remote(
            hidden_ref(kind, pos), hidden_ref(kind, target), hz_s.at[kind, target], hz_r.at[kind, target], to
        )

    def hx_copy(n, ref):
        return remote(ref, ref, hx_s.at[n], hx_r.at[n], xmate)

    def forward(kind, pos):
        if pos == 0:
            targets = ((1, ahead), (2, behind))
        elif pos % 2 == 1:
            targets = ((pos + 2, ahead),) if pos < 7 else ()
        else:
            targets = ((pos + 2, behind),) if pos < 6 else ()
        for target, to in targets:
            copy = hz_copy(kind, pos, target, to)
            copy.start()
            sent.append(copy)

    def to_xmate(pos):
        copy = hx_copy(pos, h2.at[pos, x])
        copy.start()
        sent.append(copy)

    def step_blocks(k):
        return (0, 1) if k == 0 else (2 * k - 1, 2 if k < 4 else 1)

    def mate_sums(k):
        some = pl.ds(0, step_blocks(k)[1] * 64)
        return remote(dp.at[k, 1 - core, some], dr.at[k, some], dr_s.at[k], dr_r.at[k], mate)

    def down_parts(k):
        first, count = step_blocks(k)

        def part(n):
            if n == 0:
                for pos in range(first, first + count):
                    hx_copy(pos, h2.at[pos, x_other]).wait_recv()
            c, cols = n // 2, slice(n % 2 * 256, n % 2 * 256 + 256)
            left = h1[first : first + count].reshape(count * 64, C1)
            right = h2[first : first + count].reshape(count * 64, C2)
            dp[k, c, : count * 64, cols] = jnp.dot(
                left, down_w[c, :C1, cols], preferred_element_type=F32
            ) + jnp.dot(right, down_w[c, C1:, cols], preferred_element_type=F32)
            if n == 3:
                mate_sums(k).start()
                sent.append(mate_sums(k))

        return [functools.partial(part, n) for n in range(4)]

    def return_copy(pos, owner):
        return remote(ds_send.at[pos], fr.at[g], fr_s.at[pos], fr_r.at[g], (owner, b))

    returns = []

    def return_parts(k):
        first, count = step_blocks(k)

        def part(j):
            if j == 0:
                mate_sums(k).wait_recv()
            pos = first + j
            there = count - 1 - j
            total = (
                dp[k, core, j * 64 : j * 64 + 64] + dr[k, there * 64 : there * 64 + 64]
            ).astype(BF16)
            ds_send[pos] = total
            owner = lax.rem(z + (-sign if j == 0 else sign) * k + RING, RING)
            returns.append((pos, owner))

            @pl.when(owner != g)
            def _():
                return_copy(pos, owner).start()

            @pl.when(owner == g)
            def _():
                fr[g] = total

        return [functools.partial(part, j) for j in range(count)]

    own_rows = [pl.ds(pl.multiple_of(h * 32, 32), 32) for h in (x, x_other)]

    def owner_of(k, j):
        return lax.rem(z + (-sign if j == 0 else sign) * k + RING, RING)

    def half_sums(k, n):
        size = step_blocks(k)[1] * 32
        some = pl.ds(n * size, size)
        sem = 2 * k - 3 + n
        return remote(dp.at[k, 1 - core, some], dr.at[k, some], dr_s.at[sem], dr_r.at[sem], mate)

    def half_copy(k, j, n, slot):
        pos = 2 * k - 1 + j
        return remote(
            ds_send.at[pos, own_rows[n]],
            fr.at[slot, own_rows[n]],
            fl_s.at[pos - 5, n],
            fl_r.at[n, slot],
            (owner_of(k, j), b),
        )

    def half_down(k, n):
        first, count = step_blocks(k)
        h = (x, x_other)[n]
        if n == 1:
            for pos in range(first, first + count):
                hx_copy(pos, h2.at[pos, x_other]).wait_recv()
        left = h1[first : first + count, h].reshape(count * 32, C1)
        right = h2[first : first + count, h].reshape(count * 32, C2)
        for c in range(2):
            dp[k, c, n * count * 32 : (n + 1) * count * 32] = jnp.dot(
                left, down_w[c, :C1], preferred_element_type=F32
            ) + jnp.dot(right, down_w[c, C1:], preferred_element_type=F32)
        half_sums(k, n).start()
        sent.append(half_sums(k, n))

    def half_return(k, n):
        half_sums(k, n).wait_recv()
        first, count = step_blocks(k)
        for j in range(count):
            here = (n * count + j) * 32
            there = (n * count + count - 1 - j) * 32
            total = (dp[k, core, here : here + 32] + dr[k, there : there + 32]).astype(BF16)
            ds_send[first + j, own_rows[n]] = total
            owner = owner_of(k, j)

            @pl.when(owner != g)
            def _():
                half_copy(k, j, n, g).start()

            @pl.when(owner == g)
            def _():
                fr[g, own_rows[n]] = total

    forward(2, 0)
    forward(0, 0)
    copy = hx_copy(8, h1.at[0, x])
    copy.start()
    sent.append(copy)
    to_xmate(0)
    pushes[3].wait()
    loads[2].wait()
    hx_copy(8, h1.at[0, x_other]).wait_recv()
    forward(1, 0)
    for k in range(1, 4):
        parts = down_parts(k - 1)
        if k >= 2:
            parts = return_parts(k - 2) + parts
        arrivals = [(kind, pos) for kind in (2, 0, 1) for pos in (2 * k - 1, 2 * k)]
        for n, (kind, pos) in enumerate(arrivals):
            hz_copy(kind, pos, pos, ahead).wait_recv()
            forward(kind, pos)
            if kind == 2:
                to_xmate(pos)
            lo, hi = n * len(parts) // len(arrivals), (n + 1) * len(parts) // len(arrivals)
            for part in parts[lo:hi]:
                part()
    half_down(3, 0)
    hz_copy(2, 7, 7, ahead).wait_recv()
    to_xmate(7)
    for part in return_parts(2):
        part()
    half_return(3, 0)
    hz_copy(0, 7, 7, ahead).wait_recv()
    half_down(4, 0)
    half_down(3, 1)
    half_return(4, 0)
    hz_copy(1, 7, 7, ahead).wait_recv()
    half_return(3, 1)
    half_down(4, 1)
    half_return(4, 1)

    total = wide_s[...]
    away = lax.rem(z - g + RING, RING)
    in_halves = (away >= 3) & (away <= 5)

    @pl.when(in_halves)
    def _():
        for half in range(2):
            for n in ORDER:
                half_copy(4, 0, half, source(n)).wait_recv()

    @pl.when(jnp.logical_not(in_halves))
    def _():
        for n in ORDER:
            remote(
                ds_send.at[0], fr.at[source(n)], fr_s.at[0], fr_r.at[source(n)], (peer(n), b)
            ).wait_recv()

    for j in range(GROUPS):
        total = total + fr[j].astype(F32)
    out[...] = total

    for copy in merges + gathers + to_mate:
        copy.wait_send()
    for n in range(8):
        xg_copy(n).wait_send()
    xu_copy.wait_send()
    for copy in sent:
        copy.wait_send()
    for k, j in ((3, 0), (3, 1), (4, 0)):

        @pl.when(owner_of(k, j) != g)
        def _():
            half_copy(k, j, 0, g).wait_send()
            half_copy(k, j, 1, g).wait_send()

    for pos, owner in returns:

        @pl.when(owner != g)
        def _():
            return_copy(pos, owner).wait_send()


def layer(queries, keys, values, key_new, value_new, lengths, res, gain, gate, up, down):
    vmem = pl.BlockSpec(memory_space=pltpu.VMEM)
    hbm = pl.BlockSpec(memory_space=pl.ANY)
    V = pltpu.VMEM
    dma = lambda *shape: pltpu.SemaphoreType.DMA(shape)
    scratch = [
        V((64, 2048), BF16), V((64, 64, 128), BF16), V((64, 64, 128), BF16),
        V((64, 128), BF16), V((64, 128), BF16), pltpu.SMEM((64,), jnp.int32),
        V((64, FEAT), BF16), V((FEAT,), BF16),
        V((64, 2048), F32), V((64, 128), F32), V((64, 128), F32), V((16, 64, 128), F32),
        V((128, 128), F32), V((4, 4, 64, 128), BF16), V((32, 128), F32),
        V((4, 4, 64, 128), BF16), V((128, 128), F32), V((64, FEAT), F32), V((2, 32, FEAT), BF16),
        V((2, 8, FEAT), F32),
        V((2 * FEAT, HALF), BF16), V((2 * FEAT, HALF), BF16), V((2, HALF, FEAT), BF16),
        V((8, 2, 32, 2 * FEAT), BF16), V((8, 2, 32, WIDE), F32), V((8, 2, 32, GATE), F32),
        V((8, 32, GATE), BF16), V((8, 32, GATE), BF16),
        V((4, 2, 32, WIDE), BF16), V((4, 2, 32, WIDE), BF16),
        V((3, 2, 32, WIDE), BF16), V((3, 2, 32, WIDE), BF16),
        V((4, 32, GATE), BF16), V((4, 32, GATE), BF16),
        V((3, 32, GATE), BF16), V((3, 32, GATE), BF16),
        V((32, WIDE), BF16), V((32, WIDE), BF16),
        V((8, 2, 32, C1), BF16), V((8, 2, 32, C2), BF16),
        V((5, 2, 128, FEAT), F32), V((5, 128, FEAT), F32),
        V((8, 64, FEAT), BF16), V((8, 64, FEAT), BF16),
        dma(8), dma(3), dma(4), dma(4), dma(8), dma(8), dma(8), dma(8), dma(8), dma(8),
        dma(8), dma(8), dma(4, 2), dma(4, 2), dma(3, 2), dma(3, 2),
        dma(4), dma(4), dma(3), dma(3), pltpu.SemaphoreType.DMA, pltpu.SemaphoreType.DMA,
        dma(3, 8), dma(3, 8), dma(9), dma(9), dma(7), dma(7), dma(8), dma(8), dma(3, 2), dma(2, 8),
    ]
    return pl.pallas_call(
        kernel,
        out_shape=pltpu.VMEM((64, FEAT), F32),
        in_specs=[hbm] * 11,
        out_specs=vmem,
        scratch_shapes=scratch,
        compiler_params=pltpu.CompilerParams(
            collective_id=0, has_side_effects=True, vmem_limit_bytes=61 * 1024 * 1024
        ),
        cost_estimate=pl.CostEstimate(
            flops=5_300_000_000, bytes_accessed=11_000_000, transcendentals=100_000
        ),
    )(queries, keys, values, key_new, value_new, lengths, res, gain, gate, up, down)


def on_device(
    residual_in,
    queries,
    key_cache,
    value_cache,
    key_new,
    value_new,
    lengths,
    ffn_gain,
    gate_weight,
    up_weight,
    down_weight,
):
    return layer(
        queries,
        key_cache,
        value_cache,
        key_new,
        value_new,
        lengths,
        residual_in,
        ffn_gain,
        gate_weight,
        up_weight,
        down_weight,
    )


def solution(mesh):
    in_specs = (
        P("grp", "blk"),
        P("grp", None),
        P("grp", "blk", None, None),
        P("grp", "blk", None, None),
        P("grp", None),
        P("grp", None),
        P("grp"),
        P("blk"),
        P("blk", "grp"),
        P("blk", "grp"),
        P("grp", "blk"),
    )
    out_specs = P("grp", "blk")
    return jax.shard_map(
        on_device, mesh=mesh, in_specs=in_specs, out_specs=out_specs, check_vma=False
    )
```
